32 devices in a mesh: ka: 8 (over y, x, core), pb: 4 (over z).
Axes of the slice: x: 2, y: 2, z: 4, core: 2. Of those that a mesh axis runs over, the one named last changes fastest.
Arguments:
- coupling: float32 [256, 16, 2, 64, 128], P('ka', 'pb'), may hold values from -6 to 6
- gauge: float32 [256, 64, 128], P('ka'), may hold values from -0.5 to 0.5
- kq_index: int32 [16, 256], P(None, 'ka'), may hold values from 0 to 255, as said below
- fine_coords: int32 [3, 16], replicated, may hold values from 0 to 31
- eig_right: float32 [16, 64, 128], P('ka'), may hold values from -0.5 to 0.5
- eig_left: float32 [16, 16, 64, 128], P('ka', 'pb'), may hold values from -0.5 to 0.5
- energy_k: float32 [16, 64], P('ka'), may hold values from -4 to 4
- energy_kq: float32 [16, 16, 64], P('ka', 'pb'), may hold values from -4 to 4
- occupied: int32 [16, 16, 64], P('ka', 'pb'), may hold values 0 or 1
- frequency: float32 [16, 2], P('pb'), may hold values from 0.02 to 0.12
Outputs:
- self_energy: float32 [16, 64], P('ka')
The draws below stay inside these ranges and needn't reach their ends.
Inputs may be any that keep to these rules, and one draw needn't show every extreme that they name: kq_index[q, k] is the number of the coarse point k displaced by the q-th window point's offset on the periodic 8 x 8 x 4 grid; for each q it is a permutation of the coarse points. Among the offsets are (4, 0, 0) and (0, 0, 3).
All inputs are finite; a program needn't handle non-finite values. No bound on the sum of `occupied` on one device may be relied on, other than what follows from the above.
Results may differ from the reference program's by a relative error of at most 0.0001.
Values sent between devices are 32-bit elements; how exact they have to be, the bound alone decides.
A program may use at most 128 MiB of HBM per device.

```python
import math
import jax
import jax.numpy as jnp
from jax import lax

W = 64
GX = 8
GY = 8
GZ = 4
FG = 32
NBR = 2
NK = 256
NQ = 16
NF = 16


def draw_kq_index(key, part):
    offset_first = jax.random.randint(jax.random.fold_in(key, 11), (NQ,), 0, GX)
    offset_second = jax.random.randint(jax.random.fold_in(key, 12), (NQ,), 0, GY)
    offset_third = jax.random.randint(jax.random.fold_in(key, 13), (NQ,), 0, GZ)
    offset_first = offset_first.at[0].set(GX // 2).at[1].set(0)
    offset_second = offset_second.at[0].set(0).at[1].set(0)
    offset_third = offset_third.at[0].set(0).at[1].set(GZ - 1)
    order = jax.random.permutation(jax.random.fold_in(key, 14), NQ)
    offset_first = offset_first[order][:, None]
    offset_second = offset_second[order][:, None]
    offset_third = offset_third[order][:, None]
    points = jnp.arange(NK, dtype=jnp.int32)[None, :]
    along_first = (points // (GY * GZ) + offset_first) % GX
    along_second = (points // GZ % GY + offset_second) % GY
    along_third = (points % GZ + offset_third) % GZ
    return ((along_first * GY + along_second) * GZ + along_third).astype(jnp.int32)


def touch_ends(drawn, key, smallest, top_value):
    longest = drawn.shape.index(max(drawn.shape))
    spots = []
    for shift in (0, 1):
        where = [jax.random.randint(jax.random.fold_in(key, axis), (), 0, length) for axis, length in enumerate(drawn.shape)]
        where[longest] = (where[longest] + shift) % drawn.shape[longest]
        spots.append(tuple(where))
    return drawn.at[spots[0]].set(smallest).at[spots[1]].set(top_value)


def steps_of(key, shape, pieces, least, high):
    def one(dim, parts):
        draws = jax.random.uniform(jax.random.fold_in(jax.random.fold_in(key, 6), dim), (parts,), jnp.float32, least / len(pieces), high / len(pieces))
        return jnp.repeat(jnp.exp(draws), shape[dim] // parts).reshape((-1,) + (1,) * (len(shape) - dim - 1))

    level = one(*pieces[0])
    for cut in pieces[1:]:
        level = level * one(*cut)
    return level


def scatter_about(own_key, shape, scale, reach, shards=(), kind=jnp.bfloat16):
    drawn = jax.random.normal(own_key, shape, jnp.float32) * scale
    if len(shards) > 0:
        drawn = steps_of(own_key, shape, shards, -0.22, 0.18) * drawn
    return jnp.clip(drawn, min=-reach, max=reach).astype(kind)


def setup_inputs(seed: int = 0) -> dict:
    seeds = jax.random.split(jax.random.key(seed), 11)
    coupling = scatter_about(seeds[0], (NK, NQ, NBR, W, 2 * W), 1.0, 6.0, ((0, 8), (1, 4)), jnp.float32)
    gauge = scatter_about(seeds[1], (NK, W, 2 * W), (2 * W) ** -0.5, 0.5, ((0, 8),), jnp.float32)
    kq_index = draw_kq_index(jax.random.fold_in(seeds[10], 71), 0)
    fine_coords = touch_ends(jax.random.randint(seeds[3], (3, NF), 0, FG), jax.random.fold_in(seeds[3], 1), 0, FG - 1).astype(jnp.int32)
    eig_right = scatter_about(seeds[4], (NF, W, 2 * W), (2 * W) ** -0.5, 0.5, ((0, 8),), jnp.float32)
    eig_left = scatter_about(seeds[5], (NF, NQ, W, 2 * W), (2 * W) ** -0.5, 0.5, ((0, 8), (1, 4)), jnp.float32)
    energy_k = scatter_about(seeds[6], (NF, W), 1.0, 4.0, ((0, 8),), jnp.float32)
    energy_kq = scatter_about(seeds[7], (NF, NQ, W), 1.0, 4.0, ((0, 8), (1, 4)), jnp.float32)
    occupied = touch_ends((jax.random.randint(seeds[8], (NF, NQ, W), 0, 2) < 1).astype(jnp.int32), jax.random.fold_in(seeds[8], 1), 0, 1)
    frequency = jnp.clip(jnp.exp(math.log(0.12) - 1.7917595 * jax.random.uniform(seeds[9], (NQ, NBR), jnp.float32) ** steps_of(seeds[9], (NQ, NBR), ((0, 4),), -0.2, 0.2)), 0.02, 0.12)
    return dict(coupling=coupling, gauge=gauge, kq_index=kq_index, fine_coords=fine_coords, eig_right=eig_right, eig_left=eig_left, energy_k=energy_k, energy_kq=energy_kq, occupied=occupied, frequency=frequency)


PRECISE = lax.Precision.HIGHEST
BROADEN = 0.1
THERMAL = 0.05


def product(left_matrix, right_matrix):
    return jnp.dot(left_matrix, right_matrix, precision=PRECISE, preferred_element_type=jnp.float32)


def phase_tables(fine_coords):
    points = jnp.arange(NK, dtype=jnp.int32)
    along_first = points // (GY * GZ)
    along_second = (points // GZ) % GY
    along_third = points % GZ
    cell_first = along_first - GX // 2
    cell_second = along_second - GY // 2
    cell_third = along_third - GZ // 2
    coarse_index = (cell_first[:, None] * along_first[None, :] * (GY * GZ) + cell_second[:, None] * along_second[None, :] * (GX * GZ) + cell_third[:, None] * along_third[None, :] * (GX * GY)) % NK
    coarse_angles = coarse_index.astype(jnp.float32) * (2.0 * math.pi / NK)
    fine_index = (fine_coords[0][:, None] * cell_first[None, :] + fine_coords[1][:, None] * cell_second[None, :] + fine_coords[2][:, None] * cell_third[None, :]) % FG
    fine_angles = fine_index.astype(jnp.float32) * (2.0 * math.pi / FG)
    return jnp.cos(coarse_angles) / NK, -jnp.sin(coarse_angles) / NK, jnp.cos(fine_angles), jnp.sin(fine_angles)


def right_block(matrix):
    orbitals = matrix.shape[-2]
    real_part = matrix[..., :orbitals]
    imag_part = matrix[..., orbitals:]
    upper_half = jnp.concatenate([real_part, imag_part], -1)
    lower_half = jnp.concatenate([-imag_part, real_part], -1)
    return jnp.concatenate([upper_half, lower_half], -2)


def apply_left(left_gauge, matrices, pattern):
    orbitals = left_gauge.shape[-2]
    swapped = jnp.concatenate([matrices[..., orbitals:], -matrices[..., :orbitals]], -1)
    first_term = jnp.einsum(pattern, left_gauge[..., :orbitals], matrices, precision=PRECISE)
    return first_term + jnp.einsum(pattern, left_gauge[..., orbitals:], swapped, precision=PRECISE)


def sectioned(cols_real, cols_imag, tables):
    coarse_real, coarse_imag, fine_cos, fine_sin = tables
    space_real = product(coarse_real, cols_real) - product(coarse_imag, cols_imag)
    space_imag = product(coarse_real, cols_imag) + product(coarse_imag, cols_real)
    fine_real_part = product(fine_cos, space_real) - product(fine_sin, space_imag)
    fine_imag_part = product(fine_cos, space_imag) + product(fine_sin, space_real)
    return fine_real_part, fine_imag_part


def self_terms(bloch, energy_k, energy_kq, occupied, frequency):
    orbitals = bloch.shape[-2]
    square = bloch * bloch
    strength = square[..., :orbitals] + square[..., orbitals:]
    phonon = frequency[None, :, :, None, None]
    bose_factor = 1.0 / (jnp.exp(phonon / THERMAL) - 1.0)
    filled = occupied.astype(jnp.float32)[:, :, None, :, None]
    energy_gap = energy_k[:, None, None, None, :] - energy_kq[:, :, None, :, None]
    shifted_up = energy_gap + phonon
    shifted_down = energy_gap - phonon
    kernel = (bose_factor + filled) * shifted_up / (shifted_up * shifted_up + BROADEN * BROADEN)
    kernel = kernel + (bose_factor + 1.0 - filled) * shifted_down / (shifted_down * shifted_down + BROADEN * BROADEN)
    return jnp.sum(strength / (2.0 * phonon) * kernel, axis=(1, 2, 3))


def reference(coupling, gauge, kq_index, fine_coords, eig_right, eig_left, energy_k, energy_kq, occupied, frequency):
    tables = phase_tables(fine_coords)
    gauge_block = right_block(gauge)
    fine_block = right_block(eig_right)
    orbitals = gauge.shape[1]
    branches = coupling.shape[2]
    points_fine = fine_coords.shape[1]

    def one_qpoint(qpoint, running_sum):
        coupled = lax.dynamic_index_in_dim(coupling, qpoint, 1, keepdims=False)
        targets = lax.dynamic_index_in_dim(kq_index, qpoint, 0, keepdims=False)
        partner = jnp.take(gauge, targets, axis=0)
        right_gauge = jnp.einsum('kbjc,kcd->kbjd', coupled, gauge_block, precision=PRECISE)
        wannier = apply_left(partner, right_gauge, 'kjm,kbjc->kbmc')
        columns = wannier.reshape(NK, branches, orbitals, 2, orbitals).transpose(0, 3, 1, 2, 4).reshape(NK, 2, -1)
        fine_real_part, fine_imag_part = sectioned(columns[:, 0], columns[:, 1], tables)
        fine_coupling = jnp.stack([fine_real_part, fine_imag_part], 1).reshape(points_fine, 2, branches, orbitals, orbitals)
        fine_coupling = fine_coupling.transpose(0, 2, 3, 1, 4).reshape(points_fine, branches, orbitals, 2 * orbitals)
        left_fine = lax.dynamic_index_in_dim(eig_left, qpoint, 1, keepdims=False)
        half_way = jnp.einsum('fbjc,fcd->fbjd', fine_coupling, fine_block, precision=PRECISE)
        bloch = apply_left(left_fine, half_way, 'fjm,fbjc->fbmc')
        contrib = self_terms(bloch[:, None], energy_k, lax.dynamic_slice_in_dim(energy_kq, qpoint, 1, 1), lax.dynamic_slice_in_dim(occupied, qpoint, 1, 1), lax.dynamic_slice_in_dim(frequency, qpoint, 1, 0))
        return running_sum + contrib

    summed = lax.fori_loop(0, NQ, one_qpoint, jnp.zeros((points_fine, orbitals), jnp.float32))
    return summed / (NQ * orbitals)
```

```python
import functools
import math

import jax
import jax.numpy as jnp
from jax import lax
from jax.experimental import pallas as pl
from jax.experimental.pallas import tpu as pltpu
from jax.sharding import PartitionSpec as P

GX = 8
GY = 8
GZ = 4
FG = 32
NK = 256
BROADEN = 0.1
THERMAL = 0.05
VMEM_LIMIT = 48 * 1024 * 1024


def split(value):
    high = value.astype(jnp.bfloat16)
    low = (value - high.astype(jnp.float32)).astype(jnp.bfloat16)
    return high, low


def dot(first, second):
    return jnp.dot(first, second, preferred_element_type=jnp.float32)


def swap_halves(value, low_sign):
    half = value.shape[-1] // 2
    lane = lax.broadcasted_iota(jnp.int32, value.shape, value.ndim - 1)
    rolled = pltpu.roll(value, half, value.ndim - 1)
    return jnp.where(lane < half, low_sign * rolled, -low_sign * rolled)


def right_weights(matrix):
    block = jnp.concatenate([matrix, swap_halves(matrix, -1.0)], 0)
    high, low = split(block)
    row = jnp.concatenate([high, low], 1)
    return jnp.concatenate([row, row], 0)


def right_product(rows, weights):
    high, low = split(rows)
    wide = dot(jnp.concatenate([high, low], 1), weights)
    half = wide.shape[1] // 2
    return wide[:, :half] + wide[:, half:]


def left_weights(matrix):
    high, low = split(matrix)
    turned = jnp.concatenate([high, low], 0).T
    return jnp.concatenate([turned, turned], 1)


def left_product(turned, high, low):
    wide = dot(turned, jnp.concatenate([high, high, low, low], 0))
    half = wide.shape[0] // 2
    lanes = wide.shape[1] // 2
    parts = []
    for branch in range(2):
        piece = wide[:, branch * lanes : (branch + 1) * lanes]
        parts.append(piece[:half] + swap_halves(piece[half:], 1.0))
    return parts


def right_kernel(coupling_ref, gauge_ref, out_ref):
    points, qpoints, branches, orbitals, lanes = coupling_ref.shape
    for point in range(points):
        weights = right_weights(gauge_ref[point])
        rows = coupling_ref[point].reshape(qpoints * branches * orbitals, lanes)
        product = right_product(rows, weights)
        for q in range(qpoints):
            first = product[2 * q * orbitals : (2 * q + 1) * orbitals]
            second = product[(2 * q + 1) * orbitals : (2 * q + 2) * orbitals]
            high, low = split(jnp.concatenate([first, second], 1))
            out_ref[point, q, :orbitals] = high
            out_ref[point, q, orbitals:] = low


def left_kernel(index_ref, gauge_ref, right_ref, table_ref, out_ref, held_ref):
    points = right_ref.shape[0]
    _, orbitals, padded, _ = held_ref.shape
    fine = out_ref.shape[0]
    lanes = out_ref.shape[3]

    @pl.when(pl.program_id(0) == 0)
    def _():
        if padded != points:
            held_ref[...] = jnp.zeros_like(held_ref)

        @pl.loop(0, points, unroll=min(4, points))
        def _(point):
            turned = left_weights(gauge_ref[index_ref[point]])
            block = right_ref[point, 0]
            parts = left_product(turned, block[:orbitals], block[orbitals:])
            for branch in range(2):
                held_ref[branch, :, point, :] = parts[branch]

    t_high, t_low = split(table_ref[0])
    table = jnp.concatenate([t_high, t_high, t_low, t_low], 1)

    @pl.loop(0, orbitals, unroll=8)
    def _(row):
        high, low = split(jnp.concatenate([held_ref[0, row], held_ref[1, row]], 1))
        wide = dot(table, jnp.concatenate([high, low, high, low], 0))
        for branch in range(2):
            piece = wide[:, branch * lanes : (branch + 1) * lanes]
            out_ref[:, branch, row, :] = piece[:fine] + swap_halves(piece[fine:], -1.0)


def fine_kernel(scalars_ref, coupled_ref, right_ref, left_ref, energy_ref, gap_ref, filled_ref, out_ref):
    fine, qpoints, branches, orbitals, lanes = coupled_ref.shape
    for f in range(fine):
        weights = right_weights(right_ref[f])
        rows = coupled_ref[f].reshape(qpoints * branches * orbitals, lanes)
        product = right_product(rows, weights)
        total = jnp.zeros((orbitals, lanes), jnp.float32)
        energy = energy_ref[f : f + 1, :]
        for q in range(qpoints):
            first = product[2 * q * orbitals : (2 * q + 1) * orbitals]
            second = product[(2 * q + 1) * orbitals : (2 * q + 2) * orbitals]
            high, low = split(jnp.concatenate([first, second], 1))
            parts = left_product(left_weights(left_ref[f, q]), high, low)
            difference = energy - gap_ref[f, q]
            filled = filled_ref[f, q]
            for branch in range(branches):
                phonon = scalars_ref[0, q * branches + branch]
                bose = scalars_ref[1, q * branches + branch]
                scale = scalars_ref[2, q * branches + branch]
                square = parts[branch] * parts[branch]
                up = difference + phonon
                down = difference - phonon
                kernel = (bose + filled) * up / (up * up + BROADEN * BROADEN)
                kernel = kernel + (bose + 1.0 - filled) * down / (down * down + BROADEN * BROADEN)
                total = total + square * scale * kernel
        summed = jnp.sum(total, axis=0, keepdims=True)
        out_ref[f : f + 1, :] = summed + pltpu.roll(summed, lanes // 2, 1)


def axis_table(coords, places, cells):
    cell = jnp.arange(cells, dtype=jnp.int32) - cells // 2
    shift = coords[:, None] - places[None, :] * (FG // cells)
    index = (cell[:, None, None] * shift[None]) % FG
    angles = index.astype(jnp.float32) * (2.0 * math.pi / FG)
    return jnp.sum(jnp.cos(angles), 0) / cells, jnp.sum(jnp.sin(angles), 0) / cells


def times(first, second):
    return (
        first[0] * second[0] - first[1] * second[1],
        first[0] * second[1] + first[1] * second[0],
    )


def phase_table(fine_coords, points):
    first = axis_table(fine_coords[0], points // (GY * GZ), GX)
    second = axis_table(fine_coords[1], points // GZ % GY, GY)
    third = axis_table(fine_coords[2], points % GZ, GZ)
    return times(times(first, second), third)


def shards(
    coupling,
    gauge,
    kq_index,
    fine_coords,
    eig_right,
    eig_left,
    energy_k,
    energy_kq,
    occupied,
    frequency,
):
    points, qpoints, branches, orbitals, lanes = coupling.shape
    pb_count = lax.axis_size("pb")
    fine_total = fine_coords.shape[1]
    chunk = 16 if fine_total % 16 == 0 else fine_total
    chunks = fine_total // chunk
    padded = -(-points // 16) * 16
    params = pltpu.CompilerParams(vmem_limit_bytes=VMEM_LIMIT)

    all_gauge = lax.all_gather(gauge, "ka", axis=0, tiled=True)

    step = 4 if points % 4 == 0 else 1
    right = pl.pallas_call(
        right_kernel,
        grid=(points // step,),
        in_specs=[
            pl.BlockSpec((step, qpoints, branches, orbitals, lanes), lambda i: (i, 0, 0, 0, 0)),
            pl.BlockSpec((step, orbitals, lanes), lambda i: (i, 0, 0)),
        ],
        out_specs=pl.BlockSpec((step, qpoints, 2 * orbitals, 2 * lanes), lambda i: (i, 0, 0, 0)),
        out_shape=jax.ShapeDtypeStruct((points, qpoints, 2 * orbitals, 2 * lanes), jnp.bfloat16),
        compiler_params=params,
        cost_estimate=pl.CostEstimate(
            flops=8 * coupling.size * lanes, bytes_accessed=8 * coupling.size, transcendentals=0
        ),
        name="right_gauge",
    )(coupling, gauge)

    own_points = lax.axis_index("ka") * points + jnp.arange(points, dtype=jnp.int32)
    table_real, table_imag = phase_table(fine_coords, own_points)
    table = jnp.stack([table_real, table_imag]).reshape(2, chunks, chunk, points)
    table = table.transpose(1, 0, 2, 3).reshape(chunks, 2 * chunk, points)
    table = jnp.pad(table, ((0, 0), (0, 0), (0, padded - points)))
    own_rows = lax.dynamic_slice_in_dim(kq_index, lax.axis_index("pb") * qpoints, qpoints, 0)

    def one_qpoint(index, right_part, q):
        return pl.pallas_call(
            left_kernel,
            grid=(chunks,),
            in_specs=[
                pl.BlockSpec(memory_space=pltpu.SMEM),
                pl.BlockSpec(all_gauge.shape, lambda i: (0, 0, 0), pipeline_mode=pl.Buffered(1)),
                pl.BlockSpec((points, 1, 2 * orbitals, 2 * lanes), lambda i: (0, q, 0, 0)),
                pl.BlockSpec((1, 2 * chunk, padded), lambda i: (i, 0, 0)),
            ],
            out_specs=pl.BlockSpec((chunk, branches, orbitals, lanes), lambda i: (i, 0, 0, 0)),
            out_shape=jax.ShapeDtypeStruct((fine_total, branches, orbitals, lanes), jnp.float32),
            scratch_shapes=[pltpu.VMEM((branches, orbitals, padded, lanes), jnp.float32)],
            compiler_params=params,
            cost_estimate=pl.CostEstimate(
                flops=20_000_000_000, bytes_accessed=4 * all_gauge.size, transcendentals=0
            ),
            name="left_gauge",
        )(index, all_gauge, right_part, table)

    if chunks == 1:
        gathered = [
            lax.psum_scatter(one_qpoint(own_rows[q], right, q), "ka", scatter_dimension=0, tiled=True)
            for q in range(qpoints)
        ]
        coupled = jnp.stack(gathered, 1)
    else:

        def body(q, total):
            part = lax.dynamic_slice_in_dim(right, q, 1, 1)
            index = lax.dynamic_index_in_dim(own_rows, q, 0, keepdims=False)
            piece = lax.psum_scatter(
                one_qpoint(index, part, 0), "ka", scatter_dimension=0, tiled=True
            )
            return lax.dynamic_update_slice_in_dim(total, piece[:, None], q, 1)

        coupled = lax.fori_loop(
            0,
            qpoints,
            body,
            jnp.zeros((eig_right.shape[0], qpoints, branches, orbitals, lanes), jnp.float32),
        )

    phonon = frequency.reshape(-1)
    scalars = jnp.stack([phonon, 1.0 / (jnp.exp(phonon / THERMAL) - 1.0), 1.0 / (2.0 * phonon)])
    shape = eig_left.shape
    contrib = pl.pallas_call(
        fine_kernel,
        in_specs=[pl.BlockSpec(memory_space=pltpu.SMEM)]
        + [pl.BlockSpec(memory_space=pltpu.VMEM)] * 6,
        out_specs=pl.BlockSpec(memory_space=pltpu.VMEM),
        out_shape=jax.ShapeDtypeStruct((eig_right.shape[0], lanes), jnp.float32),
        compiler_params=params,
        name="fine_terms",
    )(
        scalars,
        coupled,
        eig_right,
        eig_left,
        jnp.concatenate([energy_k, energy_k], 1),
        jnp.broadcast_to(energy_kq[..., None], shape),
        jnp.broadcast_to(occupied.astype(jnp.float32)[..., None], shape),
    )
    summed = lax.psum(contrib[:, :orbitals], "pb")
    return summed / (qpoints * pb_count * orbitals)


def solution(mesh):
    in_specs = (
        P("ka", "pb", None, None, None),
        P("ka", None, None),
        P(None, "ka"),
        P(),
        P("ka", None, None),
        P("ka", "pb", None, None),
        P("ka", None),
        P("ka", "pb", None),
        P("ka", "pb", None),
        P("pb", None),
    )
    out_specs = P("ka", None)
    return jax.shard_map(shards, mesh=mesh, in_specs=in_specs, out_specs=out_specs, check_vma=False)
```

```python
import functools
import math

import jax
import jax.numpy as jnp
from jax import lax
from jax.experimental import pallas as pl
from jax.experimental.pallas import tpu as pltpu
from jax.sharding import PartitionSpec as P

GX = 8
GY = 8
GZ = 4
FG = 32
NK = 256
BROADEN = 0.1
THERMAL = 0.05
VMEM_LIMIT = 48 * 1024 * 1024
UNROLL = 4


def split(value):
    high = value.astype(jnp.bfloat16)
    low = (value - high.astype(jnp.float32)).astype(jnp.bfloat16)
    return high, low


def dot(first, second):
    return jnp.dot(first, second, preferred_element_type=jnp.float32)


def swap_halves(value, low_sign):
    half = value.shape[-1] // 2
    lane = lax.broadcasted_iota(jnp.int32, value.shape, value.ndim - 1)
    rolled = pltpu.roll(value, half, value.ndim - 1)
    return jnp.where(lane < half, low_sign * rolled, -low_sign * rolled)


def right_weights(matrix):
    block = jnp.concatenate([matrix, swap_halves(matrix, -1.0)], 0)
    high, low = split(block)
    row = jnp.concatenate([high, low], 1)
    return jnp.concatenate([row, row], 0)


def right_product(rows, weights):
    high, low = split(rows)
    wide = dot(jnp.concatenate([high, low], 1), weights)
    half = wide.shape[1] // 2
    return wide[:, :half] + wide[:, half:]


def left_weights(matrix):
    high, low = split(matrix)
    turned = jnp.concatenate([high, low], 0).T
    return jnp.concatenate([turned, turned], 1)


def left_product(turned, high, low):
    wide = dot(turned, jnp.concatenate([high, high, low, low], 0))
    half = wide.shape[0] // 2
    lanes = wide.shape[1] // 2
    parts = []
    for branch in range(2):
        piece = wide[:, branch * lanes : (branch + 1) * lanes]
        parts.append(piece[:half] + swap_halves(piece[half:], 1.0))
    return parts


def right_kernel(coupling_ref, gauge_ref, out_ref):
    points, qpoints, branches, orbitals, lanes = coupling_ref.shape
    for point in range(points):
        weights = right_weights(gauge_ref[point])
        rows = coupling_ref[point].reshape(qpoints * branches * orbitals, lanes)
        product = right_product(rows, weights)
        for q in range(qpoints):
            first = product[2 * q * orbitals : (2 * q + 1) * orbitals]
            second = product[(2 * q + 1) * orbitals : (2 * q + 2) * orbitals]
            high, low = split(jnp.concatenate([first, second], 1))
            out_ref[point, q, :orbitals] = high
            out_ref[point, q, orbitals:] = low


def left_kernel(index_ref, gauge_ref, right_ref, table_ref, out_ref, held_ref):
    points = right_ref.shape[0]
    _, orbitals, padded, _ = held_ref.shape
    fine = out_ref.shape[0]
    lanes = out_ref.shape[3]

    @pl.when(pl.program_id(0) == 0)
    def _():
        if padded != points:
            held_ref[...] = jnp.zeros_like(held_ref)

        @pl.loop(0, points, unroll=min(4, points))
        def _(point):
            turned = left_weights(gauge_ref[index_ref[point]])
            block = right_ref[point, 0]
            parts = left_product(turned, block[:orbitals], block[orbitals:])
            for branch in range(2):
                held_ref[branch, :, point, :] = parts[branch]

    t_high, t_low = split(table_ref[0])
    table = jnp.concatenate([t_high, t_high, t_low, t_low], 1)

    @pl.loop(0, orbitals, unroll=8)
    def _(row):
        high, low = split(jnp.concatenate([held_ref[0, row], held_ref[1, row]], 1))
        wide = dot(table, jnp.concatenate([high, low, high, low], 0))
        for branch in range(2):
            piece = wide[:, branch * lanes : (branch + 1) * lanes]
            out_ref[:, branch, row, :] = piece[:fine] + swap_halves(piece[fine:], -1.0)


def fine_kernel(scalars_ref, coupled_ref, right_ref, left_ref, energy_ref, gap_ref, filled_ref, out_ref):
    fine, qpoints, branches, orbitals, lanes = coupled_ref.shape
    for f in range(fine):
        weights = right_weights(right_ref[f])
        rows = coupled_ref[f].reshape(qpoints * branches * orbitals, lanes)
        product = right_product(rows, weights)
        total = jnp.zeros((orbitals, lanes), jnp.float32)
        energy = energy_ref[f : f + 1, :]
        for q in range(qpoints):
            first = product[2 * q * orbitals : (2 * q + 1) * orbitals]
            second = product[(2 * q + 1) * orbitals : (2 * q + 2) * orbitals]
            high, low = split(jnp.concatenate([first, second], 1))
            parts = left_product(left_weights(left_ref[f, q]), high, low)
            difference = energy - gap_ref[f, q]
            filled = filled_ref[f, q]
            for branch in range(branches):
                phonon = scalars_ref[0, q * branches + branch]
                bose = scalars_ref[1, q * branches + branch]
                scale = scalars_ref[2, q * branches + branch]
                square = parts[branch] * parts[branch]
                up = difference + phonon
                down = difference - phonon
                kernel = (bose + filled) * up / (up * up + BROADEN * BROADEN)
                kernel = kernel + (bose + 1.0 - filled) * down / (down * down + BROADEN * BROADEN)
                total = total + square * scale * kernel
        summed = jnp.sum(total, axis=0, keepdims=True)
        out_ref[f : f + 1, :] = summed + pltpu.roll(summed, lanes // 2, 1)


def window_kernel(
    index_ref, scalars_ref, gauge_ref, right_ref, table_ref, fine_right_ref, fine_left_ref,
    energy_ref, gap_ref, filled_ref, out_ref,
    held_ref, partial_ref, arrived_ref, total_ref, terms_ref, others_ref,
    send_sem, recv_sem, terms_send, terms_recv,
):
    points, qpoints = right_ref.shape[0], right_ref.shape[1]
    branches, orbitals, padded, lanes = held_ref.shape
    fine_total = partial_ref.shape[1]
    fine = fine_right_ref.shape[0]
    ka_count, pb_count = lax.axis_size("ka"), lax.axis_size("pb")
    me, layer = lax.axis_index("ka"), lax.axis_index("pb")

    def ka_device(offset):
        return (lax.rem(me + offset, ka_count), layer)

    def pb_device(offset):
        return (me, lax.rem(layer + offset, pb_count))

    barrier = pltpu.get_barrier_semaphore()
    for offset in range(1, ka_count):
        pl.semaphore_signal(
            barrier, inc=1, device_id=ka_device(offset), device_id_type=pl.DeviceIdType.MESH
        )
    for offset in range(1, pb_count):
        pl.semaphore_signal(
            barrier, inc=1, device_id=pb_device(offset), device_id_type=pl.DeviceIdType.MESH
        )
    pl.semaphore_wait(barrier, ka_count + pb_count - 2)

    def piece(q, offset):
        target = lax.rem(me + offset, ka_count)
        return pltpu.make_async_remote_copy(
            src_ref=partial_ref.at[q, pl.ds(target * fine, fine)],
            dst_ref=arrived_ref.at[q, offset - 1],
            send_sem=send_sem.at[q, offset - 1],
            recv_sem=recv_sem.at[q, offset - 1],
            device_id=(target, layer),
            device_id_type=pl.DeviceIdType.MESH,
        )

    total_ref[...] = jnp.zeros_like(total_ref)
    terms_ref[...] = jnp.zeros_like(terms_ref)
    if padded != points:
        held_ref[...] = jnp.zeros_like(held_ref)

    @pl.loop(0, qpoints + 1)
    def _(q):
        @pl.when(q < qpoints)
        def _():
            @pl.loop(0, points, unroll=min(UNROLL, points))
            def _(point):
                turned = left_weights(gauge_ref[index_ref[q * points + point]])
                block = right_ref[point, q]
                parts = left_product(turned, block[:orbitals], block[orbitals:])
                for branch in range(2):
                    held_ref[branch, :, point, :] = parts[branch]

            t_high, t_low = split(table_ref[...])
            table = jnp.concatenate([t_high, t_high, t_low, t_low], 1)

            @pl.loop(0, orbitals, unroll=8)
            def _(row):
                high, low = split(jnp.concatenate([held_ref[0, row], held_ref[1, row]], 1))
                wide = dot(table, jnp.concatenate([high, low, high, low], 0))
                for branch in range(2):
                    part = wide[:, branch * lanes : (branch + 1) * lanes]
                    partial_ref[q, :, branch, row, :] = part[:fine_total] + swap_halves(
                        part[fine_total:], -1.0
                    )

            for offset in range(1, ka_count):
                piece(q, offset).start()

        @pl.when(q > 0)
        def _():
            done = q - 1
            for offset in range(1, ka_count):
                piece(done, offset).wait()
            for f in range(fine):
                rows = partial_ref[done, me * fine + f]
                for offset in range(1, ka_count):
                    rows = rows + arrived_ref[done, offset - 1, f]
                product = right_product(
                    rows.reshape(branches * orbitals, lanes), right_weights(fine_right_ref[f])
                )
                high, low = split(jnp.concatenate([product[:orbitals], product[orbitals:]], 1))
                parts = left_product(left_weights(fine_left_ref[f, done]), high, low)
                difference = energy_ref[f : f + 1, :] - gap_ref[f, done]
                filled = filled_ref[f, done]
                total = total_ref[f]
                for branch in range(branches):
                    phonon = scalars_ref[0, done * branches + branch]
                    bose = scalars_ref[1, done * branches + branch]
                    scale = scalars_ref[2, done * branches + branch]
                    square = parts[branch] * parts[branch]
                    up = difference + phonon
                    down = difference - phonon
                    kernel = (bose + filled) * up / (up * up + BROADEN * BROADEN)
                    kernel = kernel + (bose + 1.0 - filled) * down / (
                        down * down + BROADEN * BROADEN
                    )
                    total = total + square * scale * kernel
                total_ref[f] = total

    for f in range(fine):
        summed = jnp.sum(total_ref[f], axis=0, keepdims=True)
        terms_ref[f : f + 1, :] = summed + pltpu.roll(summed, lanes // 2, 1)
    copies = []
    for offset in range(1, pb_count):
        copies.append(
            pltpu.make_async_remote_copy(
                src_ref=terms_ref,
                dst_ref=others_ref.at[offset - 1],
                send_sem=terms_send.at[offset - 1],
                recv_sem=terms_recv.at[offset - 1],
                device_id=pb_device(offset),
                device_id_type=pl.DeviceIdType.MESH,
            )
        )
        copies[-1].start()
    summed = terms_ref[...]
    for offset in range(1, pb_count):
        copies[offset - 1].wait()
        summed = summed + others_ref[offset - 1]
    out_ref[...] = summed[:fine] / (qpoints * pb_count * orbitals)


def axis_table(coords, places, cells):
    cell = jnp.arange(cells, dtype=jnp.int32) - cells // 2
    shift = coords[:, None] - places[None, :] * (FG // cells)
    index = (cell[:, None, None] * shift[None]) % FG
    angles = index.astype(jnp.float32) * (2.0 * math.pi / FG)
    return jnp.sum(jnp.cos(angles), 0) / cells, jnp.sum(jnp.sin(angles), 0) / cells


def times(first, second):
    return (
        first[0] * second[0] - first[1] * second[1],
        first[0] * second[1] + first[1] * second[0],
    )


def phase_table(fine_coords, points):
    first = axis_table(fine_coords[0], points // (GY * GZ), GX)
    second = axis_table(fine_coords[1], points // GZ % GY, GY)
    third = axis_table(fine_coords[2], points % GZ, GZ)
    return times(times(first, second), third)


def shards(
    coupling,
    gauge,
    kq_index,
    fine_coords,
    eig_right,
    eig_left,
    energy_k,
    energy_kq,
    occupied,
    frequency,
):
    points, qpoints, branches, orbitals, lanes = coupling.shape
    pb_count = lax.axis_size("pb")
    fine_total = fine_coords.shape[1]
    chunk = 16 if fine_total % 16 == 0 else fine_total
    chunks = fine_total // chunk
    padded = -(-points // 16) * 16
    params = pltpu.CompilerParams(vmem_limit_bytes=VMEM_LIMIT)

    all_gauge = lax.all_gather(gauge, "ka", axis=0, tiled=True)

    step = 4 if points % 4 == 0 else 1
    right = pl.pallas_call(
        right_kernel,
        grid=(points // step,),
        in_specs=[
            pl.BlockSpec((step, qpoints, branches, orbitals, lanes), lambda i: (i, 0, 0, 0, 0)),
            pl.BlockSpec((step, orbitals, lanes), lambda i: (i, 0, 0)),
        ],
        out_specs=pl.BlockSpec((step, qpoints, 2 * orbitals, 2 * lanes), lambda i: (i, 0, 0, 0)),
        out_shape=jax.ShapeDtypeStruct((points, qpoints, 2 * orbitals, 2 * lanes), jnp.bfloat16),
        compiler_params=params,
        cost_estimate=pl.CostEstimate(
            flops=8 * coupling.size * lanes, bytes_accessed=8 * coupling.size, transcendentals=0
        ),
        name="right_gauge",
    )(coupling, gauge)

    own_points = lax.axis_index("ka") * points + jnp.arange(points, dtype=jnp.int32)
    table_real, table_imag = phase_table(fine_coords, own_points)
    table = jnp.stack([table_real, table_imag]).reshape(2, chunks, chunk, points)
    table = table.transpose(1, 0, 2, 3).reshape(chunks, 2 * chunk, points)
    table = jnp.pad(table, ((0, 0), (0, 0), (0, padded - points)))
    own_rows = lax.dynamic_slice_in_dim(kq_index, lax.axis_index("pb") * qpoints, qpoints, 0)

    phonon = frequency.reshape(-1)
    scalars = jnp.stack([phonon, 1.0 / (jnp.exp(phonon / THERMAL) - 1.0), 1.0 / (2.0 * phonon)])
    shape = eig_left.shape
    energy_lanes = jnp.concatenate([energy_k, energy_k], 1)
    gap_lanes = jnp.broadcast_to(energy_kq[..., None], shape)
    filled_lanes = jnp.broadcast_to(occupied.astype(jnp.float32)[..., None], shape)

    ka_count = lax.axis_size("ka")
    fine_rows = eig_right.shape[0]
    fine_rows_padded = -(-fine_rows // 8) * 8
    partial_size = fine_total * branches * orbitals * lanes * 4 * qpoints
    if chunks == 1 and ka_count > 1 and pb_count > 1 and partial_size <= 8 * 1024 * 1024:
        ka_others, pb_others = ka_count - 1, pb_count - 1
        vmem = pl.BlockSpec(memory_space=pltpu.VMEM)
        smem = pl.BlockSpec(memory_space=pltpu.SMEM)
        summed = pl.pallas_call(
            window_kernel,
            in_specs=[smem, smem] + [vmem] * 8,
            out_specs=vmem,
            out_shape=jax.ShapeDtypeStruct((fine_rows, lanes), jnp.float32),
            scratch_shapes=[
                pltpu.VMEM((branches, orbitals, padded, lanes), jnp.float32),
                pltpu.VMEM((qpoints, fine_total, branches, orbitals, lanes), jnp.float32),
                pltpu.VMEM((qpoints, ka_others, fine_rows, branches, orbitals, lanes), jnp.float32),
                pltpu.VMEM((fine_rows, orbitals, lanes), jnp.float32),
                pltpu.VMEM((fine_rows_padded, lanes), jnp.float32),
                pltpu.VMEM((pb_others, fine_rows_padded, lanes), jnp.float32),
                pltpu.SemaphoreType.DMA((qpoints, ka_others)),
                pltpu.SemaphoreType.DMA((qpoints, ka_others)),
                pltpu.SemaphoreType.DMA((pb_others,)),
                pltpu.SemaphoreType.DMA((pb_others,)),
            ],
            compiler_params=pltpu.CompilerParams(
                vmem_limit_bytes=VMEM_LIMIT, collective_id=0, has_side_effects=True
            ),
            name="window",
        )(
            own_rows.reshape(-1), scalars, all_gauge, right, table[0], eig_right, eig_left,
            energy_lanes, gap_lanes, filled_lanes,
        )
        return summed[:, :orbitals]

    def one_qpoint(index, right_part, q):
        return pl.pallas_call(
            left_kernel,
            grid=(chunks,),
            in_specs=[
                pl.BlockSpec(memory_space=pltpu.SMEM),
                pl.BlockSpec(all_gauge.shape, lambda i: (0, 0, 0), pipeline_mode=pl.Buffered(1)),
                pl.BlockSpec((points, 1, 2 * orbitals, 2 * lanes), lambda i: (0, q, 0, 0)),
                pl.BlockSpec((1, 2 * chunk, padded), lambda i: (i, 0, 0)),
            ],
            out_specs=pl.BlockSpec((chunk, branches, orbitals, lanes), lambda i: (i, 0, 0, 0)),
            out_shape=jax.ShapeDtypeStruct((fine_total, branches, orbitals, lanes), jnp.float32),
            scratch_shapes=[pltpu.VMEM((branches, orbitals, padded, lanes), jnp.float32)],
            compiler_params=params,
            cost_estimate=pl.CostEstimate(
                flops=20_000_000_000, bytes_accessed=4 * all_gauge.size, transcendentals=0
            ),
            name="left_gauge",
        )(index, all_gauge, right_part, table)

    if chunks == 1:
        gathered = [
            lax.psum_scatter(one_qpoint(own_rows[q], right, q), "ka", scatter_dimension=0, tiled=True)
            for q in range(qpoints)
        ]
        coupled = jnp.stack(gathered, 1)
    else:

        def body(q, total):
            part = lax.dynamic_slice_in_dim(right, q, 1, 1)
            index = lax.dynamic_index_in_dim(own_rows, q, 0, keepdims=False)
            piece = lax.psum_scatter(
                one_qpoint(index, part, 0), "ka", scatter_dimension=0, tiled=True
            )
            return lax.dynamic_update_slice_in_dim(total, piece[:, None], q, 1)

        coupled = lax.fori_loop(
            0,
            qpoints,
            body,
            jnp.zeros((eig_right.shape[0], qpoints, branches, orbitals, lanes), jnp.float32),
        )

    contrib = pl.pallas_call(
        fine_kernel,
        in_specs=[pl.BlockSpec(memory_space=pltpu.SMEM)]
        + [pl.BlockSpec(memory_space=pltpu.VMEM)] * 6,
        out_specs=pl.BlockSpec(memory_space=pltpu.VMEM),
        out_shape=jax.ShapeDtypeStruct((eig_right.shape[0], lanes), jnp.float32),
        compiler_params=params,
        name="fine_terms",
    )(
        scalars,
        coupled,
        eig_right,
        eig_left,
        energy_lanes,
        gap_lanes,
        filled_lanes,
    )
    summed = lax.psum(contrib[:, :orbitals], "pb")
    return summed / (qpoints * pb_count * orbitals)


def solution(mesh):
    in_specs = (
        P("ka", "pb", None, None, None),
        P("ka", None, None),
        P(None, "ka"),
        P(),
        P("ka", None, None),
        P("ka", "pb", None, None),
        P("ka", None),
        P("ka", "pb", None),
        P("ka", "pb", None),
        P("pb", None),
    )
    out_specs = P("ka", None)
    return jax.shard_map(shards, mesh=mesh, in_specs=in_specs, out_specs=out_specs, check_vma=False)
```

```python
import functools
import math

import jax
import jax.numpy as jnp
from jax import lax
from jax.experimental import pallas as pl
from jax.experimental.pallas import tpu as pltpu
from jax.sharding import PartitionSpec as P

GX = 8
GY = 8
GZ = 4
FG = 32
NK = 256
BROADEN = 0.1
THERMAL = 0.05
VMEM_LIMIT = 48 * 1024 * 1024
UNROLL = 4


def split(value):
    high = value.astype(jnp.bfloat16)
    low = (value - high.astype(jnp.float32)).astype(jnp.bfloat16)
    return high, low


def dot(first, second):
    return jnp.dot(first, second, preferred_element_type=jnp.float32)


def swap_halves(value, low_sign):
    half = value.shape[-1] // 2
    lane = lax.broadcasted_iota(jnp.int32, value.shape, value.ndim - 1)
    rolled = pltpu.roll(value, half, value.ndim - 1)
    return jnp.where(lane < half, low_sign * rolled, -low_sign * rolled)


def right_weights(matrix):
    block = jnp.concatenate([matrix, swap_halves(matrix, -1.0)], 0)
    high, low = split(block)
    row = jnp.concatenate([high, low], 1)
    return jnp.concatenate([row, row], 0)


def right_product(rows, weights):
    high, low = split(rows)
    wide = dot(jnp.concatenate([high, low], 1), weights)
    half = wide.shape[1] // 2
    return wide[:, :half] + wide[:, half:]


def left_weights(matrix):
    high, low = split(matrix)
    turned = jnp.concatenate([high, low], 0).T
    return jnp.concatenate([turned, turned], 1)


def left_product(turned, high, low):
    wide = dot(turned, jnp.concatenate([high, high, low, low], 0))
    half = wide.shape[0] // 2
    lanes = wide.shape[1] // 2
    parts = []
    for branch in range(2):
        piece = wide[:, branch * lanes : (branch + 1) * lanes]
        parts.append(piece[:half] + swap_halves(piece[half:], 1.0))
    return parts


def right_kernel(coupling_ref, gauge_ref, out_ref):
    points, qpoints, branches, orbitals, lanes = coupling_ref.shape
    for point in range(points):
        weights = right_weights(gauge_ref[point])
        rows = coupling_ref[point].reshape(qpoints * branches * orbitals, lanes)
        product = right_product(rows, weights)
        for q in range(qpoints):
            first = product[2 * q * orbitals : (2 * q + 1) * orbitals]
            second = product[(2 * q + 1) * orbitals : (2 * q + 2) * orbitals]
            high, low = split(jnp.concatenate([first, second], 1))
            out_ref[point, q, :orbitals] = high
            out_ref[point, q, orbitals:] = low


def left_kernel(index_ref, gauge_ref, right_ref, table_ref, out_ref, held_ref):
    points = right_ref.shape[0]
    _, orbitals, padded, _ = held_ref.shape
    fine = out_ref.shape[0]
    lanes = out_ref.shape[3]

    @pl.when(pl.program_id(0) == 0)
    def _():
        if padded != points:
            held_ref[...] = jnp.zeros_like(held_ref)

        @pl.loop(0, points, unroll=min(4, points))
        def _(point):
            turned = left_weights(gauge_ref[index_ref[point]])
            block = right_ref[point, 0]
            parts = left_product(turned, block[:orbitals], block[orbitals:])
            for branch in range(2):
                held_ref[branch, :, point, :] = parts[branch]

    t_high, t_low = split(table_ref[0])
    table = jnp.concatenate([t_high, t_high, t_low, t_low], 1)

    @pl.loop(0, orbitals, unroll=8)
    def _(row):
        high, low = split(jnp.concatenate([held_ref[0, row], held_ref[1, row]], 1))
        wide = dot(table, jnp.concatenate([high, low, high, low], 0))
        for branch in range(2):
            piece = wide[:, branch * lanes : (branch + 1) * lanes]
            out_ref[:, branch, row, :] = piece[:fine] + swap_halves(piece[fine:], -1.0)


def fine_kernel(scalars_ref, coupled_ref, right_ref, left_ref, energy_ref, gap_ref, filled_ref, out_ref):
    fine, qpoints, branches, orbitals, lanes = coupled_ref.shape
    for f in range(fine):
        weights = right_weights(right_ref[f])
        rows = coupled_ref[f].reshape(qpoints * branches * orbitals, lanes)
        product = right_product(rows, weights)
        total = jnp.zeros((orbitals, lanes), jnp.float32)
        energy = energy_ref[f : f + 1, :]
        for q in range(qpoints):
            first = product[2 * q * orbitals : (2 * q + 1) * orbitals]
            second = product[(2 * q + 1) * orbitals : (2 * q + 2) * orbitals]
            high, low = split(jnp.concatenate([first, second], 1))
            parts = left_product(left_weights(left_ref[f, q]), high, low)
            difference = energy - gap_ref[f, q]
            filled = filled_ref[f, q]
            for branch in range(branches):
                phonon = scalars_ref[0, q * branches + branch]
                bose = scalars_ref[1, q * branches + branch]
                scale = scalars_ref[2, q * branches + branch]
                square = parts[branch] * parts[branch]
                up = difference + phonon
                down = difference - phonon
                kernel = (bose + filled) * up / (up * up + BROADEN * BROADEN)
                kernel = kernel + (bose + 1.0 - filled) * down / (down * down + BROADEN * BROADEN)
                total = total + square * scale * kernel
        summed = jnp.sum(total, axis=0, keepdims=True)
        out_ref[f : f + 1, :] = summed + pltpu.roll(summed, lanes // 2, 1)


def window_kernel(
    index_ref, scalars_ref, own_ref, coupling_ref, table_ref, fine_right_ref, fine_left_ref,
    energy_ref, gap_ref, filled_ref, out_ref,
    held_ref, partial_ref, arrived_ref, total_ref, terms_ref, others_ref,
    send_sem, recv_sem, terms_send, terms_recv,
    gauge_ref, coupled_ref, right_ref, gather_send, gather_recv, load_sem,
):
    load = pltpu.make_async_copy(coupling_ref, coupled_ref, load_sem)
    load.start()
    points, qpoints = right_ref.shape[0], right_ref.shape[1]
    branches, orbitals, padded, lanes = held_ref.shape
    fine_total = partial_ref.shape[1]
    fine = fine_right_ref.shape[0]
    ka_count, pb_count = lax.axis_size("ka"), lax.axis_size("pb")
    me, layer = lax.axis_index("ka"), lax.axis_index("pb")

    def ka_device(offset):
        return (lax.rem(me + offset, ka_count), layer)

    def pb_device(offset):
        return (me, lax.rem(layer + offset, pb_count))

    gauge_ref[pl.ds(me * points, points)] = own_ref[...]
    barrier = pltpu.get_barrier_semaphore()
    for offset in range(1, ka_count):
        pl.semaphore_signal(
            barrier, inc=1, device_id=ka_device(offset), device_id_type=pl.DeviceIdType.MESH
        )
    for offset in range(1, pb_count):
        pl.semaphore_signal(
            barrier, inc=1, device_id=pb_device(offset), device_id_type=pl.DeviceIdType.MESH
        )
    pl.semaphore_wait(barrier, ka_count + pb_count - 2)

    bits = [1 << b for b in range(1, ka_count.bit_length() - 1)]
    orders = (bits + [1], bits[::-1] + [1])
    half = points // 2

    def last_bit(stream, mask):
        return [bit for bit in orders[stream] if mask & bit][-1]

    def flipped(mask):
        place = me
        for bit in orders[0]:
            if mask & bit:
                place = place + bit - 2 * bit * lax.rem(me // bit, 2)
        return place

    def block(stream, mask):
        bit = last_bit(stream, mask)
        rows = pl.ds(flipped(mask - bit) * points + stream * half, half)
        return pltpu.make_async_remote_copy(
            src_ref=gauge_ref.at[rows],
            dst_ref=gauge_ref.at[rows],
            send_sem=gather_send.at[stream, mask - 1],
            recv_sem=gather_recv.at[stream, mask - 1],
            device_id=(flipped(bit), layer),
            device_id_type=pl.DeviceIdType.MESH,
        )

    def forward(stream, mask):
        for bit in orders[stream]:
            later = mask | bit
            if later != mask and last_bit(stream, later) == bit:
                block(stream, later).start()

    for place in range(len(bits) + 1):
        for stream in range(2):
            block(stream, orders[stream][place]).start()

    load.wait()

    @pl.loop(0, points, unroll=2)
    def _(point):
        rows = coupled_ref[point].reshape(qpoints * branches * orbitals, lanes)
        product = right_product(rows, right_weights(own_ref[point]))
        for q in range(qpoints):
            first = product[2 * q * orbitals : (2 * q + 1) * orbitals]
            second = product[(2 * q + 1) * orbitals : (2 * q + 2) * orbitals]
            high, low = split(jnp.concatenate([first, second], 1))
            right_ref[point, q, :orbitals] = high
            right_ref[point, q, orbitals:] = low

    masks = sorted(range(1, ka_count), key=lambda mask: (mask.bit_count(), mask & 1, mask))
    for mask in masks:
        for stream in range(2):
            block(stream, mask).wait_recv()
            forward(stream, mask)
    for mask in masks:
        for stream in range(2):
            block(stream, mask).wait_send()

    def piece(q, offset):
        target = lax.rem(me + offset, ka_count)
        return pltpu.make_async_remote_copy(
            src_ref=partial_ref.at[q, pl.ds(target * fine, fine)],
            dst_ref=arrived_ref.at[q, offset - 1],
            send_sem=send_sem.at[q, offset - 1],
            recv_sem=recv_sem.at[q, offset - 1],
            device_id=(target, layer),
            device_id_type=pl.DeviceIdType.MESH,
        )

    total_ref[...] = jnp.zeros_like(total_ref)
    terms_ref[...] = jnp.zeros_like(terms_ref)
    if padded != points:
        held_ref[...] = jnp.zeros_like(held_ref)

    @pl.loop(0, qpoints + 1)
    def _(q):
        @pl.when(q < qpoints)
        def _():
            @pl.loop(0, points, unroll=min(UNROLL, points))
            def _(point):
                turned = left_weights(gauge_ref[index_ref[q * points + point]])
                parts = left_product(turned, right_ref[point, q, :orbitals], right_ref[point, q, orbitals:])
                for branch in range(2):
                    held_ref[branch, :, point, :] = parts[branch]

            t_high, t_low = split(table_ref[...])
            table = jnp.concatenate([t_high, t_high, t_low, t_low], 1)

            @pl.loop(0, orbitals, unroll=8)
            def _(row):
                high, low = split(jnp.concatenate([held_ref[0, row], held_ref[1, row]], 1))
                wide = dot(table, jnp.concatenate([high, low, high, low], 0))
                for branch in range(2):
                    part = wide[:, branch * lanes : (branch + 1) * lanes]
                    partial_ref[q, :, branch, row, :] = part[:fine_total] + swap_halves(
                        part[fine_total:], -1.0
                    )

            for offset in range(1, ka_count):
                piece(q, offset).start()

        @pl.when(q > 0)
        def _():
            done = q - 1
            for offset in range(1, ka_count):
                piece(done, offset).wait()
            for f in range(fine):
                rows = partial_ref[done, me * fine + f]
                for offset in range(1, ka_count):
                    rows = rows + arrived_ref[done, offset - 1, f]
                product = right_product(
                    rows.reshape(branches * orbitals, lanes), right_weights(fine_right_ref[f])
                )
                high, low = split(jnp.concatenate([product[:orbitals], product[orbitals:]], 1))
                parts = left_product(left_weights(fine_left_ref[f, done]), high, low)
                difference = energy_ref[f : f + 1, :] - gap_ref[f, done]
                filled = filled_ref[f, done]
                total = total_ref[f]
                for branch in range(branches):
                    phonon = scalars_ref[0, done * branches + branch]
                    bose = scalars_ref[1, done * branches + branch]
                    scale = scalars_ref[2, done * branches + branch]
                    square = parts[branch] * parts[branch]
                    up = difference + phonon
                    down = difference - phonon
                    kernel = (bose + filled) * up / (up * up + BROADEN * BROADEN)
                    kernel = kernel + (bose + 1.0 - filled) * down / (
                        down * down + BROADEN * BROADEN
                    )
                    total = total + square * scale * kernel
                total_ref[f] = total

    for f in range(fine):
        summed = jnp.sum(total_ref[f], axis=0, keepdims=True)
        terms_ref[f : f + 1, :] = summed + pltpu.roll(summed, lanes // 2, 1)
    copies = []
    for offset in range(1, pb_count):
        copies.append(
            pltpu.make_async_remote_copy(
                src_ref=terms_ref,
                dst_ref=others_ref.at[offset - 1],
                send_sem=terms_send.at[offset - 1],
                recv_sem=terms_recv.at[offset - 1],
                device_id=pb_device(offset),
                device_id_type=pl.DeviceIdType.MESH,
            )
        )
        copies[-1].start()
    summed = terms_ref[...]
    for offset in range(1, pb_count):
        copies[offset - 1].wait()
        summed = summed + others_ref[offset - 1]
    out_ref[...] = summed[:fine] / (qpoints * pb_count * orbitals)


def axis_table(coords, places, cells):
    cell = jnp.arange(cells, dtype=jnp.int32) - cells // 2
    shift = coords[:, None] - places[None, :] * (FG // cells)
    index = (cell[:, None, None] * shift[None]) % FG
    angles = index.astype(jnp.float32) * (2.0 * math.pi / FG)
    return jnp.sum(jnp.cos(angles), 0) / cells, jnp.sum(jnp.sin(angles), 0) / cells


def times(first, second):
    return (
        first[0] * second[0] - first[1] * second[1],
        first[0] * second[1] + first[1] * second[0],
    )


def phase_table(fine_coords, points):
    first = axis_table(fine_coords[0], points // (GY * GZ), GX)
    second = axis_table(fine_coords[1], points // GZ % GY, GY)
    third = axis_table(fine_coords[2], points % GZ, GZ)
    return times(times(first, second), third)


def shards(
    coupling,
    gauge,
    kq_index,
    fine_coords,
    eig_right,
    eig_left,
    energy_k,
    energy_kq,
    occupied,
    frequency,
):
    points, qpoints, branches, orbitals, lanes = coupling.shape
    pb_count = lax.axis_size("pb")
    fine_total = fine_coords.shape[1]
    chunk = 16 if fine_total % 16 == 0 else fine_total
    chunks = fine_total // chunk
    padded = -(-points // 16) * 16
    params = pltpu.CompilerParams(vmem_limit_bytes=VMEM_LIMIT)

    all_gauge = lax.all_gather(gauge, "ka", axis=0, tiled=True)

    step = 4 if points % 4 == 0 else 1
    right = pl.pallas_call(
        right_kernel,
        grid=(points // step,),
        in_specs=[
            pl.BlockSpec((step, qpoints, branches, orbitals, lanes), lambda i: (i, 0, 0, 0, 0)),
            pl.BlockSpec((step, orbitals, lanes), lambda i: (i, 0, 0)),
        ],
        out_specs=pl.BlockSpec((step, qpoints, 2 * orbitals, 2 * lanes), lambda i: (i, 0, 0, 0)),
        out_shape=jax.ShapeDtypeStruct((points, qpoints, 2 * orbitals, 2 * lanes), jnp.bfloat16),
        compiler_params=params,
        cost_estimate=pl.CostEstimate(
            flops=8 * coupling.size * lanes, bytes_accessed=8 * coupling.size, transcendentals=0
        ),
        name="right_gauge",
    )(coupling, gauge)

    own_points = lax.axis_index("ka") * points + jnp.arange(points, dtype=jnp.int32)
    table_real, table_imag = phase_table(fine_coords, own_points)
    table = jnp.stack([table_real, table_imag]).reshape(2, chunks, chunk, points)
    table = table.transpose(1, 0, 2, 3).reshape(chunks, 2 * chunk, points)
    table = jnp.pad(table, ((0, 0), (0, 0), (0, padded - points)))
    own_rows = lax.dynamic_slice_in_dim(kq_index, lax.axis_index("pb") * qpoints, qpoints, 0)

    phonon = frequency.reshape(-1)
    scalars = jnp.stack([phonon, 1.0 / (jnp.exp(phonon / THERMAL) - 1.0), 1.0 / (2.0 * phonon)])
    shape = eig_left.shape
    energy_lanes = jnp.concatenate([energy_k, energy_k], 1)
    gap_lanes = jnp.broadcast_to(energy_kq[..., None], shape)
    filled_lanes = jnp.broadcast_to(occupied.astype(jnp.float32)[..., None], shape)

    ka_count = lax.axis_size("ka")
    fine_rows = eig_right.shape[0]
    fine_rows_padded = -(-fine_rows // 8) * 8
    partial_size = fine_total * branches * orbitals * lanes * 4 * qpoints
    power = ka_count & (ka_count - 1) == 0 and points % 2 == 0
    if chunks == 1 and power and ka_count > 1 and pb_count > 1 and partial_size <= 8 * 1024 * 1024:
        ka_others, pb_others = ka_count - 1, pb_count - 1
        vmem = pl.BlockSpec(memory_space=pltpu.VMEM)
        smem = pl.BlockSpec(memory_space=pltpu.SMEM)
        summed = pl.pallas_call(
            window_kernel,
            in_specs=[smem, smem, vmem, pl.BlockSpec(memory_space=pl.ANY)] + [vmem] * 6,
            out_specs=vmem,
            out_shape=jax.ShapeDtypeStruct((fine_rows, lanes), jnp.float32),
            scratch_shapes=[
                pltpu.VMEM((branches, orbitals, padded, lanes), jnp.float32),
                pltpu.VMEM((qpoints, fine_total, branches, orbitals, lanes), jnp.float32),
                pltpu.VMEM((qpoints, ka_others, fine_rows, branches, orbitals, lanes), jnp.float32),
                pltpu.VMEM((fine_rows, orbitals, lanes), jnp.float32),
                pltpu.VMEM((fine_rows_padded, lanes), jnp.float32),
                pltpu.VMEM((pb_others, fine_rows_padded, lanes), jnp.float32),
                pltpu.SemaphoreType.DMA((qpoints, ka_others)),
                pltpu.SemaphoreType.DMA((qpoints, ka_others)),
                pltpu.SemaphoreType.DMA((pb_others,)),
                pltpu.SemaphoreType.DMA((pb_others,)),
                pltpu.VMEM((ka_count * points, orbitals, lanes), jnp.float32),
                pltpu.VMEM(coupling.shape, jnp.float32),
                pltpu.VMEM((points, qpoints, 2 * orbitals, 2 * lanes), jnp.bfloat16),
                pltpu.SemaphoreType.DMA((2, ka_others)),
                pltpu.SemaphoreType.DMA((2, ka_others)),
                pltpu.SemaphoreType.DMA,
            ],
            compiler_params=pltpu.CompilerParams(
                vmem_limit_bytes=VMEM_LIMIT, collective_id=0, has_side_effects=True
            ),
            name="window",
        )(
            own_rows.reshape(-1), scalars, gauge, coupling, table[0], eig_right, eig_left,
            energy_lanes, gap_lanes, filled_lanes,
        )
        return summed[:, :orbitals]

    def one_qpoint(index, right_part, q):
        return pl.pallas_call(
            left_kernel,
            grid=(chunks,),
            in_specs=[
                pl.BlockSpec(memory_space=pltpu.SMEM),
                pl.BlockSpec(all_gauge.shape, lambda i: (0, 0, 0), pipeline_mode=pl.Buffered(1)),
                pl.BlockSpec((points, 1, 2 * orbitals, 2 * lanes), lambda i: (0, q, 0, 0)),
                pl.BlockSpec((1, 2 * chunk, padded), lambda i: (i, 0, 0)),
            ],
            out_specs=pl.BlockSpec((chunk, branches, orbitals, lanes), lambda i: (i, 0, 0, 0)),
            out_shape=jax.ShapeDtypeStruct((fine_total, branches, orbitals, lanes), jnp.float32),
            scratch_shapes=[pltpu.VMEM((branches, orbitals, padded, lanes), jnp.float32)],
            compiler_params=params,
            cost_estimate=pl.CostEstimate(
                flops=20_000_000_000, bytes_accessed=4 * all_gauge.size, transcendentals=0
            ),
            name="left_gauge",
        )(index, all_gauge, right_part, table)

    if chunks == 1:
        gathered = [
            lax.psum_scatter(one_qpoint(own_rows[q], right, q), "ka", scatter_dimension=0, tiled=True)
            for q in range(qpoints)
        ]
        coupled = jnp.stack(gathered, 1)
    else:

        def body(q, total):
            part = lax.dynamic_slice_in_dim(right, q, 1, 1)
            index = lax.dynamic_index_in_dim(own_rows, q, 0, keepdims=False)
            piece = lax.psum_scatter(
                one_qpoint(index, part, 0), "ka", scatter_dimension=0, tiled=True
            )
            return lax.dynamic_update_slice_in_dim(total, piece[:, None], q, 1)

        coupled = lax.fori_loop(
            0,
            qpoints,
            body,
            jnp.zeros((eig_right.shape[0], qpoints, branches, orbitals, lanes), jnp.float32),
        )

    contrib = pl.pallas_call(
        fine_kernel,
        in_specs=[pl.BlockSpec(memory_space=pltpu.SMEM)]
        + [pl.BlockSpec(memory_space=pltpu.VMEM)] * 6,
        out_specs=pl.BlockSpec(memory_space=pltpu.VMEM),
        out_shape=jax.ShapeDtypeStruct((eig_right.shape[0], lanes), jnp.float32),
        compiler_params=params,
        name="fine_terms",
    )(
        scalars,
        coupled,
        eig_right,
        eig_left,
        energy_lanes,
        gap_lanes,
        filled_lanes,
    )
    summed = lax.psum(contrib[:, :orbitals], "pb")
    return summed / (qpoints * pb_count * orbitals)


def solution(mesh):
    in_specs = (
        P("ka", "pb", None, None, None),
        P("ka", None, None),
        P(None, "ka"),
        P(),
        P("ka", None, None),
        P("ka", "pb", None, None),
        P("ka", None),
        P("ka", "pb", None),
        P("ka", "pb", None),
        P("pb", None),
    )
    out_specs = P("ka", None)
    return jax.shard_map(shards, mesh=mesh, in_specs=in_specs, out_specs=out_specs, check_vma=False)
```

```python
import functools
import math

import jax
import jax.numpy as jnp
from jax import lax
from jax.experimental import pallas as pl
from jax.experimental.pallas import tpu as pltpu
from jax.sharding import PartitionSpec as P

GX = 8
GY = 8
GZ = 4
FG = 32
NK = 256
BROADEN = 0.1
THERMAL = 0.05
VMEM_LIMIT = 56 * 1024 * 1024
UNROLL = 4


def split(value):
    high = value.astype(jnp.bfloat16)
    low = (value - high.astype(jnp.float32)).astype(jnp.bfloat16)
    return high, low


def dot(first, second):
    return jnp.dot(first, second, preferred_element_type=jnp.float32)


def swap_halves(value, low_sign):
    half = value.shape[-1] // 2
    lane = lax.broadcasted_iota(jnp.int32, value.shape, value.ndim - 1)
    rolled = pltpu.roll(value, half, value.ndim - 1)
    return jnp.where(lane < half, low_sign * rolled, -low_sign * rolled)


def right_weights(matrix):
    block = jnp.concatenate([matrix, swap_halves(matrix, -1.0)], 0)
    high, low = split(block)
    row = jnp.concatenate([high, low], 1)
    return jnp.concatenate([row, row], 0)


def right_product(rows, weights):
    high, low = split(rows)
    wide = dot(jnp.concatenate([high, low], 1), weights)
    half = wide.shape[1] // 2
    return wide[:, :half] + wide[:, half:]


def left_weights(matrix):
    high, low = split(matrix)
    turned = jnp.concatenate([high, low], 0).T
    return jnp.concatenate([turned, turned], 1)


def left_product(turned, high, low):
    wide = dot(turned, jnp.concatenate([high, high, low, low], 0))
    half = wide.shape[0] // 2
    lanes = wide.shape[1] // 2
    parts = []
    for branch in range(2):
        piece = wide[:, branch * lanes : (branch + 1) * lanes]
        parts.append(piece[:half] + swap_halves(piece[half:], 1.0))
    return parts


def right_kernel(coupling_ref, gauge_ref, out_ref):
    points, qpoints, branches, orbitals, lanes = coupling_ref.shape
    for point in range(points):
        weights = right_weights(gauge_ref[point])
        rows = coupling_ref[point].reshape(qpoints * branches * orbitals, lanes)
        product = right_product(rows, weights)
        for q in range(qpoints):
            first = product[2 * q * orbitals : (2 * q + 1) * orbitals]
            second = product[(2 * q + 1) * orbitals : (2 * q + 2) * orbitals]
            high, low = split(jnp.concatenate([first, second], 1))
            out_ref[point, q, :orbitals] = high
            out_ref[point, q, orbitals:] = low


def left_kernel(index_ref, gauge_ref, right_ref, table_ref, out_ref, held_ref):
    points = right_ref.shape[0]
    _, orbitals, padded, _ = held_ref.shape
    fine = out_ref.shape[0]
    lanes = out_ref.shape[3]

    @pl.when(pl.program_id(0) == 0)
    def _():
        if padded != points:
            held_ref[...] = jnp.zeros_like(held_ref)

        @pl.loop(0, points, unroll=min(4, points))
        def _(point):
            turned = left_weights(gauge_ref[index_ref[point]])
            block = right_ref[point, 0]
            parts = left_product(turned, block[:orbitals], block[orbitals:])
            for branch in range(2):
                held_ref[branch, :, point, :] = parts[branch]

    t_high, t_low = split(table_ref[0])
    table = jnp.concatenate([t_high, t_high, t_low, t_low], 1)

    @pl.loop(0, orbitals, unroll=8)
    def _(row):
        high, low = split(jnp.concatenate([held_ref[0, row], held_ref[1, row]], 1))
        wide = dot(table, jnp.concatenate([high, low, high, low], 0))
        for branch in range(2):
            piece = wide[:, branch * lanes : (branch + 1) * lanes]
            out_ref[:, branch, row, :] = piece[:fine] + swap_halves(piece[fine:], -1.0)


def fine_kernel(scalars_ref, coupled_ref, right_ref, left_ref, energy_ref, gap_ref, filled_ref, out_ref):
    fine, qpoints, branches, orbitals, lanes = coupled_ref.shape
    for f in range(fine):
        weights = right_weights(right_ref[f])
        rows = coupled_ref[f].reshape(qpoints * branches * orbitals, lanes)
        product = right_product(rows, weights)
        total = jnp.zeros((orbitals, lanes), jnp.float32)
        energy = energy_ref[f : f + 1, :]
        for q in range(qpoints):
            first = product[2 * q * orbitals : (2 * q + 1) * orbitals]
            second = product[(2 * q + 1) * orbitals : (2 * q + 2) * orbitals]
            high, low = split(jnp.concatenate([first, second], 1))
            parts = left_product(left_weights(left_ref[f, q]), high, low)
            difference = energy - gap_ref[f, q]
            filled = filled_ref[f, q]
            for branch in range(branches):
                phonon = scalars_ref[0, q * branches + branch]
                bose = scalars_ref[1, q * branches + branch]
                scale = scalars_ref[2, q * branches + branch]
                square = parts[branch] * parts[branch]
                up = difference + phonon
                down = difference - phonon
                kernel = (bose + filled) * up / (up * up + BROADEN * BROADEN)
                kernel = kernel + (bose + 1.0 - filled) * down / (down * down + BROADEN * BROADEN)
                total = total + square * scale * kernel
        summed = jnp.sum(total, axis=0, keepdims=True)
        out_ref[f : f + 1, :] = summed + pltpu.roll(summed, lanes // 2, 1)


def window_kernel(
    index_ref, scalars_ref, own_ref, coupling_ref, table_ref, fine_right_ref, fine_left_ref,
    energy_ref, gap_ref, filled_ref, out_ref,
    held_ref, partial_ref, arrived_ref, total_ref, terms_ref, others_ref,
    send_sem, recv_sem, terms_send, terms_recv,
    gauge_ref, coupled_ref, right_ref, gather_send, gather_recv, load_sem, turned_ref,
):
    load = pltpu.make_async_copy(coupling_ref, coupled_ref, load_sem)
    load.start()
    points, qpoints = right_ref.shape[0], right_ref.shape[1]
    branches, orbitals, padded, lanes = held_ref.shape
    fine_total = partial_ref.shape[1]
    fine = fine_right_ref.shape[0]
    ka_count, pb_count = lax.axis_size("ka"), lax.axis_size("pb")
    me, layer = lax.axis_index("ka"), lax.axis_index("pb")

    def ka_device(offset):
        return (lax.rem(me + offset, ka_count), layer)

    def pb_device(offset):
        return (me, lax.rem(layer + offset, pb_count))

    gauge_ref[pl.ds(me * points, points)] = own_ref[...]
    barrier = pltpu.get_barrier_semaphore()
    for offset in range(1, ka_count):
        pl.semaphore_signal(
            barrier, inc=1, device_id=ka_device(offset), device_id_type=pl.DeviceIdType.MESH
        )
    for offset in range(1, pb_count):
        pl.semaphore_signal(
            barrier, inc=1, device_id=pb_device(offset), device_id_type=pl.DeviceIdType.MESH
        )
    pl.semaphore_wait(barrier, ka_count + pb_count - 2)

    bits = [1 << b for b in range(1, ka_count.bit_length() - 1)]
    orders = (bits + [1], bits[::-1] + [1])
    half = points // 2

    def last_bit(stream, mask):
        return [bit for bit in orders[stream] if mask & bit][-1]

    def flipped(mask):
        place = me
        for bit in orders[0]:
            if mask & bit:
                place = place + bit - 2 * bit * lax.rem(me // bit, 2)
        return place

    def block(stream, mask):
        bit = last_bit(stream, mask)
        rows = pl.ds(flipped(mask - bit) * points + stream * half, half)
        return pltpu.make_async_remote_copy(
            src_ref=gauge_ref.at[rows],
            dst_ref=gauge_ref.at[rows],
            send_sem=gather_send.at[stream, mask - 1],
            recv_sem=gather_recv.at[stream, mask - 1],
            device_id=(flipped(bit), layer),
            device_id_type=pl.DeviceIdType.MESH,
        )

    def forward(stream, mask):
        for bit in orders[stream]:
            later = mask | bit
            if later != mask and last_bit(stream, later) == bit:
                block(stream, later).start()

    for place in range(len(bits) + 1):
        for stream in range(2):
            block(stream, orders[stream][place]).start()

    load.wait()

    @pl.loop(0, points, unroll=2)
    def _(point):
        rows = coupled_ref[point].reshape(qpoints * branches * orbitals, lanes)
        product = right_product(rows, right_weights(own_ref[point]))
        for q in range(qpoints):
            first = product[2 * q * orbitals : (2 * q + 1) * orbitals]
            second = product[(2 * q + 1) * orbitals : (2 * q + 2) * orbitals]
            high, low = split(jnp.concatenate([first, second], 1))
            right_ref[point, q, :orbitals] = high
            right_ref[point, q, orbitals:] = low

    def turn(mask):
        start = flipped(mask) * points

        @pl.loop(0, points, unroll=min(UNROLL, points))
        def _(point):
            high, low = split(gauge_ref[start + point])
            turned_ref[start + point] = jnp.concatenate([high, low], 0).T

    def arrive(masks):
        for mask in masks:
            for stream in range(2):
                block(stream, mask).wait_recv()
                forward(stream, mask)

    turn(0)
    arrive([1])
    turn(1)
    for count in range(1, len(bits) + 1):
        group = [mask for mask in range(2, ka_count, 2) if mask.bit_count() == count]
        arrive(group)
        for mask in group:
            turn(mask)
        for mask in group:
            arrive([mask + 1])
            turn(mask + 1)
    for mask in range(1, ka_count):
        for stream in range(2):
            block(stream, mask).wait_send()

    def piece(q, offset):
        target = lax.rem(me + offset, ka_count)
        return pltpu.make_async_remote_copy(
            src_ref=partial_ref.at[q, pl.ds(target * fine, fine)],
            dst_ref=arrived_ref.at[q, offset - 1],
            send_sem=send_sem.at[q, offset - 1],
            recv_sem=recv_sem.at[q, offset - 1],
            device_id=(target, layer),
            device_id_type=pl.DeviceIdType.MESH,
        )

    total_ref[...] = jnp.zeros_like(total_ref)
    terms_ref[...] = jnp.zeros_like(terms_ref)
    if padded != points:
        held_ref[...] = jnp.zeros_like(held_ref)

    @pl.loop(0, qpoints + 1)
    def _(q):
        @pl.when(q < qpoints)
        def _():
            @pl.loop(0, points, unroll=min(UNROLL, points))
            def _(point):
                turned = turned_ref[index_ref[q * points + point]]
                turned = jnp.concatenate([turned, turned], 1)
                parts = left_product(turned, right_ref[point, q, :orbitals], right_ref[point, q, orbitals:])
                for branch in range(2):
                    held_ref[branch, :, point, :] = parts[branch]

            t_high, t_low = split(table_ref[...])
            table = jnp.concatenate([t_high, t_high, t_low, t_low], 1)

            @pl.loop(0, orbitals, unroll=8)
            def _(row):
                high, low = split(jnp.concatenate([held_ref[0, row], held_ref[1, row]], 1))
                wide = dot(table, jnp.concatenate([high, low, high, low], 0))
                for branch in range(2):
                    part = wide[:, branch * lanes : (branch + 1) * lanes]
                    partial_ref[q, :, branch, row, :] = part[:fine_total] + swap_halves(
                        part[fine_total:], -1.0
                    )

            for offset in range(1, ka_count):
                piece(q, offset).start()

        @pl.when(q > 0)
        def _():
            done = q - 1
            for offset in range(1, ka_count):
                piece(done, offset).wait()
            for f in range(fine):
                rows = partial_ref[done, me * fine + f]
                for offset in range(1, ka_count):
                    rows = rows + arrived_ref[done, offset - 1, f]
                product = right_product(
                    rows.reshape(branches * orbitals, lanes), right_weights(fine_right_ref[f])
                )
                high, low = split(jnp.concatenate([product[:orbitals], product[orbitals:]], 1))
                parts = left_product(left_weights(fine_left_ref[f, done]), high, low)
                difference = energy_ref[f : f + 1, :] - gap_ref[f, done]
                filled = filled_ref[f, done]
                total = total_ref[f]
                for branch in range(branches):
                    phonon = scalars_ref[0, done * branches + branch]
                    bose = scalars_ref[1, done * branches + branch]
                    scale = scalars_ref[2, done * branches + branch]
                    square = parts[branch] * parts[branch]
                    up = difference + phonon
                    down = difference - phonon
                    kernel = (bose + filled) * up / (up * up + BROADEN * BROADEN)
                    kernel = kernel + (bose + 1.0 - filled) * down / (
                        down * down + BROADEN * BROADEN
                    )
                    total = total + square * scale * kernel
                total_ref[f] = total

    for f in range(fine):
        summed = jnp.sum(total_ref[f], axis=0, keepdims=True)
        terms_ref[f : f + 1, :] = summed + pltpu.roll(summed, lanes // 2, 1)
    copies = []
    for offset in range(1, pb_count):
        copies.append(
            pltpu.make_async_remote_copy(
                src_ref=terms_ref,
                dst_ref=others_ref.at[offset - 1],
                send_sem=terms_send.at[offset - 1],
                recv_sem=terms_recv.at[offset - 1],
                device_id=pb_device(offset),
                device_id_type=pl.DeviceIdType.MESH,
            )
        )
        copies[-1].start()
    summed = terms_ref[...]
    for offset in range(1, pb_count):
        copies[offset - 1].wait()
        summed = summed + others_ref[offset - 1]
    out_ref[...] = summed[:fine] / (qpoints * pb_count * orbitals)


def axis_table(coords, places, cells):
    cell = jnp.arange(cells, dtype=jnp.int32) - cells // 2
    shift = coords[:, None] - places[None, :] * (FG // cells)
    index = (cell[:, None, None] * shift[None]) % FG
    angles = index.astype(jnp.float32) * (2.0 * math.pi / FG)
    return jnp.sum(jnp.cos(angles), 0) / cells, jnp.sum(jnp.sin(angles), 0) / cells


def times(first, second):
    return (
        first[0] * second[0] - first[1] * second[1],
        first[0] * second[1] + first[1] * second[0],
    )


def phase_table(fine_coords, points):
    first = axis_table(fine_coords[0], points // (GY * GZ), GX)
    second = axis_table(fine_coords[1], points // GZ % GY, GY)
    third = axis_table(fine_coords[2], points % GZ, GZ)
    return times(times(first, second), third)


def shards(
    coupling,
    gauge,
    kq_index,
    fine_coords,
    eig_right,
    eig_left,
    energy_k,
    energy_kq,
    occupied,
    frequency,
):
    points, qpoints, branches, orbitals, lanes = coupling.shape
    pb_count = lax.axis_size("pb")
    fine_total = fine_coords.shape[1]
    chunk = 16 if fine_total % 16 == 0 else fine_total
    chunks = fine_total // chunk
    padded = -(-points // 16) * 16
    params = pltpu.CompilerParams(vmem_limit_bytes=VMEM_LIMIT)

    all_gauge = lax.all_gather(gauge, "ka", axis=0, tiled=True)

    step = 4 if points % 4 == 0 else 1
    right = pl.pallas_call(
        right_kernel,
        grid=(points // step,),
        in_specs=[
            pl.BlockSpec((step, qpoints, branches, orbitals, lanes), lambda i: (i, 0, 0, 0, 0)),
            pl.BlockSpec((step, orbitals, lanes), lambda i: (i, 0, 0)),
        ],
        out_specs=pl.BlockSpec((step, qpoints, 2 * orbitals, 2 * lanes), lambda i: (i, 0, 0, 0)),
        out_shape=jax.ShapeDtypeStruct((points, qpoints, 2 * orbitals, 2 * lanes), jnp.bfloat16),
        compiler_params=params,
        cost_estimate=pl.CostEstimate(
            flops=8 * coupling.size * lanes, bytes_accessed=8 * coupling.size, transcendentals=0
        ),
        name="right_gauge",
    )(coupling, gauge)

    own_points = lax.axis_index("ka") * points + jnp.arange(points, dtype=jnp.int32)
    table_real, table_imag = phase_table(fine_coords, own_points)
    table = jnp.stack([table_real, table_imag]).reshape(2, chunks, chunk, points)
    table = table.transpose(1, 0, 2, 3).reshape(chunks, 2 * chunk, points)
    table = jnp.pad(table, ((0, 0), (0, 0), (0, padded - points)))
    own_rows = lax.dynamic_slice_in_dim(kq_index, lax.axis_index("pb") * qpoints, qpoints, 0)

    phonon = frequency.reshape(-1)
    scalars = jnp.stack([phonon, 1.0 / (jnp.exp(phonon / THERMAL) - 1.0), 1.0 / (2.0 * phonon)])
    shape = eig_left.shape
    energy_lanes = jnp.concatenate([energy_k, energy_k], 1)
    gap_lanes = jnp.broadcast_to(energy_kq[..., None], shape)
    filled_lanes = jnp.broadcast_to(occupied.astype(jnp.float32)[..., None], shape)

    ka_count = lax.axis_size("ka")
    fine_rows = eig_right.shape[0]
    fine_rows_padded = -(-fine_rows // 8) * 8
    partial_size = fine_total * branches * orbitals * lanes * 4 * qpoints
    power = ka_count & (ka_count - 1) == 0 and points % 2 == 0
    if chunks == 1 and power and ka_count > 1 and pb_count > 1 and partial_size <= 8 * 1024 * 1024:
        ka_others, pb_others = ka_count - 1, pb_count - 1
        vmem = pl.BlockSpec(memory_space=pltpu.VMEM)
        smem = pl.BlockSpec(memory_space=pltpu.SMEM)
        summed = pl.pallas_call(
            window_kernel,
            in_specs=[smem, smem, vmem, pl.BlockSpec(memory_space=pl.ANY)] + [vmem] * 6,
            out_specs=vmem,
            out_shape=jax.ShapeDtypeStruct((fine_rows, lanes), jnp.float32),
            scratch_shapes=[
                pltpu.VMEM((branches, orbitals, padded, lanes), jnp.float32),
                pltpu.VMEM((qpoints, fine_total, branches, orbitals, lanes), jnp.float32),
                pltpu.VMEM((qpoints, ka_others, fine_rows, branches, orbitals, lanes), jnp.float32),
                pltpu.VMEM((fine_rows, orbitals, lanes), jnp.float32),
                pltpu.VMEM((fine_rows_padded, lanes), jnp.float32),
                pltpu.VMEM((pb_others, fine_rows_padded, lanes), jnp.float32),
                pltpu.SemaphoreType.DMA((qpoints, ka_others)),
                pltpu.SemaphoreType.DMA((qpoints, ka_others)),
                pltpu.SemaphoreType.DMA((pb_others,)),
                pltpu.SemaphoreType.DMA((pb_others,)),
                pltpu.VMEM((ka_count * points, orbitals, lanes), jnp.float32),
                pltpu.VMEM(coupling.shape, jnp.float32),
                pltpu.VMEM((points, qpoints, 2 * orbitals, 2 * lanes), jnp.bfloat16),
                pltpu.SemaphoreType.DMA((2, ka_others)),
                pltpu.SemaphoreType.DMA((2, ka_others)),
                pltpu.SemaphoreType.DMA,
                pltpu.VMEM((ka_count * points, 2 * orbitals, lanes), jnp.bfloat16),
            ],
            compiler_params=pltpu.CompilerParams(
                vmem_limit_bytes=VMEM_LIMIT, collective_id=0, has_side_effects=True
            ),
            name="window",
        )(
            own_rows.reshape(-1), scalars, gauge, coupling, table[0], eig_right, eig_left,
            energy_lanes, gap_lanes, filled_lanes,
        )
        return summed[:, :orbitals]

    def one_qpoint(index, right_part, q):
        return pl.pallas_call(
            left_kernel,
            grid=(chunks,),
            in_specs=[
                pl.BlockSpec(memory_space=pltpu.SMEM),
                pl.BlockSpec(all_gauge.shape, lambda i: (0, 0, 0), pipeline_mode=pl.Buffered(1)),
                pl.BlockSpec((points, 1, 2 * orbitals, 2 * lanes), lambda i: (0, q, 0, 0)),
                pl.BlockSpec((1, 2 * chunk, padded), lambda i: (i, 0, 0)),
            ],
            out_specs=pl.BlockSpec((chunk, branches, orbitals, lanes), lambda i: (i, 0, 0, 0)),
            out_shape=jax.ShapeDtypeStruct((fine_total, branches, orbitals, lanes), jnp.float32),
            scratch_shapes=[pltpu.VMEM((branches, orbitals, padded, lanes), jnp.float32)],
            compiler_params=params,
            cost_estimate=pl.CostEstimate(
                flops=20_000_000_000, bytes_accessed=4 * all_gauge.size, transcendentals=0
            ),
            name="left_gauge",
        )(index, all_gauge, right_part, table)

    if chunks == 1:
        gathered = [
            lax.psum_scatter(one_qpoint(own_rows[q], right, q), "ka", scatter_dimension=0, tiled=True)
            for q in range(qpoints)
        ]
        coupled = jnp.stack(gathered, 1)
    else:

        def body(q, total):
            part = lax.dynamic_slice_in_dim(right, q, 1, 1)
            index = lax.dynamic_index_in_dim(own_rows, q, 0, keepdims=False)
            piece = lax.psum_scatter(
                one_qpoint(index, part, 0), "ka", scatter_dimension=0, tiled=True
            )
            return lax.dynamic_update_slice_in_dim(total, piece[:, None], q, 1)

        coupled = lax.fori_loop(
            0,
            qpoints,
            body,
            jnp.zeros((eig_right.shape[0], qpoints, branches, orbitals, lanes), jnp.float32),
        )

    contrib = pl.pallas_call(
        fine_kernel,
        in_specs=[pl.BlockSpec(memory_space=pltpu.SMEM)]
        + [pl.BlockSpec(memory_space=pltpu.VMEM)] * 6,
        out_specs=pl.BlockSpec(memory_space=pltpu.VMEM),
        out_shape=jax.ShapeDtypeStruct((eig_right.shape[0], lanes), jnp.float32),
        compiler_params=params,
        name="fine_terms",
    )(
        scalars,
        coupled,
        eig_right,
        eig_left,
        energy_lanes,
        gap_lanes,
        filled_lanes,
    )
    summed = lax.psum(contrib[:, :orbitals], "pb")
    return summed / (qpoints * pb_count * orbitals)


def solution(mesh):
    in_specs = (
        P("ka", "pb", None, None, None),
        P("ka", None, None),
        P(None, "ka"),
        P(),
        P("ka", None, None),
        P("ka", "pb", None, None),
        P("ka", None),
        P("ka", "pb", None),
        P("ka", "pb", None),
        P("pb", None),
    )
    out_specs = P("ka", None)
    return jax.shard_map(shards, mesh=mesh, in_specs=in_specs, out_specs=out_specs, check_vma=False)
```

```python
import functools
import math

import jax
import jax.numpy as jnp
from jax import lax
from jax.experimental import pallas as pl
from jax.experimental.pallas import tpu as pltpu
from jax.sharding import PartitionSpec as P

GX = 8
GY = 8
GZ = 4
FG = 32
NK = 256
BROADEN = 0.1
THERMAL = 0.05
VMEM_LIMIT = 48 * 1024 * 1024
UNROLL = 4


def split(value):
    high = value.astype(jnp.bfloat16)
    low = (value - high.astype(jnp.float32)).astype(jnp.bfloat16)
    return high, low


def dot(first, second):
    return jnp.dot(first, second, preferred_element_type=jnp.float32)


def swap_halves(value, low_sign):
    half = value.shape[-1] // 2
    lane = lax.broadcasted_iota(jnp.int32, value.shape, value.ndim - 1)
    rolled = pltpu.roll(value, half, value.ndim - 1)
    return jnp.where(lane < half, low_sign * rolled, -low_sign * rolled)


def right_weights(matrix):
    block = jnp.concatenate([matrix, swap_halves(matrix, -1.0)], 0)
    high, low = split(block)
    row = jnp.concatenate([high, low], 1)
    return jnp.concatenate([row, row], 0)


def right_product(rows, weights):
    high, low = split(rows)
    wide = dot(jnp.concatenate([high, low], 1), weights)
    half = wide.shape[1] // 2
    return wide[:, :half] + wide[:, half:]


def left_weights(matrix):
    high, low = split(matrix)
    turned = jnp.concatenate([high, low], 0).T
    return jnp.concatenate([turned, turned], 1)


def left_product(turned, high, low):
    wide = dot(turned, jnp.concatenate([high, high, low, low], 0))
    half = wide.shape[0] // 2
    lanes = wide.shape[1] // 2
    parts = []
    for branch in range(2):
        piece = wide[:, branch * lanes : (branch + 1) * lanes]
        parts.append(piece[:half] + swap_halves(piece[half:], 1.0))
    return parts


def right_kernel(coupling_ref, gauge_ref, out_ref):
    points, qpoints, branches, orbitals, lanes = coupling_ref.shape
    for point in range(points):
        weights = right_weights(gauge_ref[point])
        rows = coupling_ref[point].reshape(qpoints * branches * orbitals, lanes)
        product = right_product(rows, weights)
        for q in range(qpoints):
            first = product[2 * q * orbitals : (2 * q + 1) * orbitals]
            second = product[(2 * q + 1) * orbitals : (2 * q + 2) * orbitals]
            high, low = split(jnp.concatenate([first, second], 1))
            out_ref[point, q, :orbitals] = high
            out_ref[point, q, orbitals:] = low


def left_kernel(index_ref, gauge_ref, right_ref, table_ref, out_ref, held_ref):
    points = right_ref.shape[0]
    _, orbitals, padded, _ = held_ref.shape
    fine = out_ref.shape[0]
    lanes = out_ref.shape[3]

    @pl.when(pl.program_id(0) == 0)
    def _():
        if padded != points:
            held_ref[...] = jnp.zeros_like(held_ref)

        @pl.loop(0, points, unroll=min(4, points))
        def _(point):
            turned = left_weights(gauge_ref[index_ref[point]])
            block = right_ref[point, 0]
            parts = left_product(turned, block[:orbitals], block[orbitals:])
            for branch in range(2):
                held_ref[branch, :, point, :] = parts[branch]

    t_high, t_low = split(table_ref[0])
    table = jnp.concatenate([t_high, t_high, t_low, t_low], 1)

    @pl.loop(0, orbitals, unroll=8)
    def _(row):
        high, low = split(jnp.concatenate([held_ref[0, row], held_ref[1, row]], 1))
        wide = dot(table, jnp.concatenate([high, low, high, low], 0))
        for branch in range(2):
            piece = wide[:, branch * lanes : (branch + 1) * lanes]
            out_ref[:, branch, row, :] = piece[:fine] + swap_halves(piece[fine:], -1.0)


def fine_kernel(scalars_ref, coupled_ref, right_ref, left_ref, energy_ref, gap_ref, filled_ref, out_ref):
    fine, qpoints, branches, orbitals, lanes = coupled_ref.shape
    for f in range(fine):
        weights = right_weights(right_ref[f])
        rows = coupled_ref[f].reshape(qpoints * branches * orbitals, lanes)
        product = right_product(rows, weights)
        total = jnp.zeros((orbitals, lanes), jnp.float32)
        energy = energy_ref[f : f + 1, :]
        for q in range(qpoints):
            first = product[2 * q * orbitals : (2 * q + 1) * orbitals]
            second = product[(2 * q + 1) * orbitals : (2 * q + 2) * orbitals]
            high, low = split(jnp.concatenate([first, second], 1))
            parts = left_product(left_weights(left_ref[f, q]), high, low)
            difference = energy - gap_ref[f, q]
            filled = filled_ref[f, q]
            for branch in range(branches):
                phonon = scalars_ref[0, q * branches + branch]
                bose = scalars_ref[1, q * branches + branch]
                scale = scalars_ref[2, q * branches + branch]
                square = parts[branch] * parts[branch]
                up = difference + phonon
                down = difference - phonon
                kernel = (bose + filled) * up / (up * up + BROADEN * BROADEN)
                kernel = kernel + (bose + 1.0 - filled) * down / (down * down + BROADEN * BROADEN)
                total = total + square * scale * kernel
        summed = jnp.sum(total, axis=0, keepdims=True)
        out_ref[f : f + 1, :] = summed + pltpu.roll(summed, lanes // 2, 1)


def window_kernel(
    index_ref, scalars_ref, own_ref, coupling_ref, table_ref, fine_right_ref, fine_left_ref,
    energy_ref, gap_ref, filled_ref, out_ref,
    held_ref, partial_ref, arrived_ref, total_ref, terms_ref, others_ref,
    send_sem, recv_sem, terms_send, terms_recv,
    gauge_ref, coupled_ref, right_ref, gather_send, gather_recv, load_sem, handed_ref, handed_send, handed_recv,
):
    load = pltpu.make_async_copy(coupling_ref, coupled_ref, load_sem)
    load.start()
    points, qpoints = right_ref.shape[0], right_ref.shape[1]
    branches, orbitals, padded, lanes = held_ref.shape
    fine_total = partial_ref.shape[1]
    fine = fine_right_ref.shape[0]
    ka_count, pb_count = lax.axis_size("ka"), lax.axis_size("pb")
    me, layer = lax.axis_index("ka"), lax.axis_index("pb")

    def ka_device(offset):
        return (lax.rem(me + offset, ka_count), layer)

    def pb_device(offset):
        return (me, lax.rem(layer + offset, pb_count))

    gauge_ref[pl.ds(me * points, points)] = own_ref[...]
    barrier = pltpu.get_barrier_semaphore()
    for offset in range(1, ka_count):
        pl.semaphore_signal(
            barrier, inc=1, device_id=ka_device(offset), device_id_type=pl.DeviceIdType.MESH
        )
    for offset in range(1, pb_count):
        pl.semaphore_signal(
            barrier, inc=1, device_id=pb_device(offset), device_id_type=pl.DeviceIdType.MESH
        )
    pl.semaphore_wait(barrier, ka_count + pb_count - 2)

    bits = [1 << b for b in range(1, ka_count.bit_length() - 1)]
    orders = (bits + [1], bits[::-1] + [1])
    half = points // 2

    def last_bit(stream, mask):
        return [bit for bit in orders[stream] if mask & bit][-1]

    def flipped(mask):
        place = me
        for bit in orders[0]:
            if mask & bit:
                place = place + bit - 2 * bit * lax.rem(me // bit, 2)
        return place

    def block(stream, mask):
        bit = last_bit(stream, mask)
        rows = pl.ds(flipped(mask - bit) * points + stream * half, half)
        return pltpu.make_async_remote_copy(
            src_ref=gauge_ref.at[rows],
            dst_ref=gauge_ref.at[rows],
            send_sem=gather_send.at[stream, mask - 1],
            recv_sem=gather_recv.at[stream, mask - 1],
            device_id=(flipped(bit), layer),
            device_id_type=pl.DeviceIdType.MESH,
        )

    def forward(stream, mask):
        for bit in orders[stream]:
            later = mask | bit
            if later != mask and last_bit(stream, later) == bit:
                block(stream, later).start()

    for place in range(len(bits) + 1):
        for stream in range(2):
            block(stream, orders[stream][place]).start()

    load.wait()

    @pl.loop(0, points, unroll=2)
    def _(point):
        rows = coupled_ref[point].reshape(qpoints * branches * orbitals, lanes)
        product = right_product(rows, right_weights(own_ref[point]))
        for q in range(qpoints):
            first = product[2 * q * orbitals : (2 * q + 1) * orbitals]
            second = product[(2 * q + 1) * orbitals : (2 * q + 2) * orbitals]
            high, low = split(jnp.concatenate([first, second], 1))
            right_ref[point, q, :orbitals] = high
            right_ref[point, q, orbitals:] = low

    masks = sorted(range(1, ka_count), key=lambda mask: (mask.bit_count(), mask & 1, mask))
    for mask in masks:
        for stream in range(2):
            block(stream, mask).wait_recv()
            forward(stream, mask)
    for mask in masks:
        for stream in range(2):
            block(stream, mask).wait_send()

    sibling = me + 1 - 2 * lax.rem(me, 2)
    pairs = ka_count // 2

    def owned(device, step):
        return lax.rem(device + 2 * step, ka_count)

    def handed(q, step):
        return pltpu.make_async_remote_copy(
            src_ref=partial_ref.at[q, pl.ds(owned(sibling, step) * fine, fine)],
            dst_ref=handed_ref.at[q, step],
            send_sem=handed_send.at[q, step],
            recv_sem=handed_recv.at[q, step],
            device_id=(sibling, layer),
            device_id_type=pl.DeviceIdType.MESH,
        )

    def piece(q, step):
        target = owned(me, step)
        return pltpu.make_async_remote_copy(
            src_ref=partial_ref.at[q, pl.ds(target * fine, fine)],
            dst_ref=arrived_ref.at[q, step - 1],
            send_sem=send_sem.at[q, step - 1],
            recv_sem=recv_sem.at[q, step - 1],
            device_id=(target, layer),
            device_id_type=pl.DeviceIdType.MESH,
        )

    total_ref[...] = jnp.zeros_like(total_ref)
    terms_ref[...] = jnp.zeros_like(terms_ref)
    if padded != points:
        held_ref[...] = jnp.zeros_like(held_ref)

    @pl.loop(0, qpoints + 2)
    def _(q):
        @pl.when(q < qpoints)
        def _():
            @pl.loop(0, points, unroll=min(UNROLL, points))
            def _(point):
                turned = left_weights(gauge_ref[index_ref[q * points + point]])
                parts = left_product(turned, right_ref[point, q, :orbitals], right_ref[point, q, orbitals:])
                for branch in range(2):
                    held_ref[branch, :, point, :] = parts[branch]

            t_high, t_low = split(table_ref[...])
            table = jnp.concatenate([t_high, t_high, t_low, t_low], 1)

            @pl.loop(0, orbitals, unroll=8)
            def _(row):
                high, low = split(jnp.concatenate([held_ref[0, row], held_ref[1, row]], 1))
                wide = dot(table, jnp.concatenate([high, low, high, low], 0))
                for branch in range(2):
                    part = wide[:, branch * lanes : (branch + 1) * lanes]
                    partial_ref[q, :, branch, row, :] = part[:fine_total] + swap_halves(
                        part[fine_total:], -1.0
                    )

            for step in range(pairs):
                handed(q, step).start()

        @pl.when((q > 0) & (q < qpoints + 1))
        def _():
            last = q - 1
            for step in range(pairs):
                handed(last, step).wait()
            for step in list(range(1, pairs)) + [0]:
                rows = pl.ds(owned(me, step) * fine, fine)
                partial_ref[last, rows] = partial_ref[last, rows] + handed_ref[last, step]
                if step > 0:
                    piece(last, step).start()

        @pl.when(q > 1)
        def _():
            done = q - 2
            for step in range(1, pairs):
                piece(done, step).wait()
            for f in range(fine):
                rows = partial_ref[done, me * fine + f]
                for step in range(1, pairs):
                    rows = rows + arrived_ref[done, step - 1, f]
                product = right_product(
                    rows.reshape(branches * orbitals, lanes), right_weights(fine_right_ref[f])
                )
                high, low = split(jnp.concatenate([product[:orbitals], product[orbitals:]], 1))
                parts = left_product(left_weights(fine_left_ref[f, done]), high, low)
                difference = energy_ref[f : f + 1, :] - gap_ref[f, done]
                filled = filled_ref[f, done]
                total = total_ref[f]
                for branch in range(branches):
                    phonon = scalars_ref[0, done * branches + branch]
                    bose = scalars_ref[1, done * branches + branch]
                    scale = scalars_ref[2, done * branches + branch]
                    square = parts[branch] * parts[branch]
                    up = difference + phonon
                    down = difference - phonon
                    kernel = (bose + filled) * up / (up * up + BROADEN * BROADEN)
                    kernel = kernel + (bose + 1.0 - filled) * down / (
                        down * down + BROADEN * BROADEN
                    )
                    total = total + square * scale * kernel
                total_ref[f] = total

    for f in range(fine):
        summed = jnp.sum(total_ref[f], axis=0, keepdims=True)
        terms_ref[f : f + 1, :] = summed + pltpu.roll(summed, lanes // 2, 1)
    copies = []
    for offset in range(1, pb_count):
        copies.append(
            pltpu.make_async_remote_copy(
                src_ref=terms_ref,
                dst_ref=others_ref.at[offset - 1],
                send_sem=terms_send.at[offset - 1],
                recv_sem=terms_recv.at[offset - 1],
                device_id=pb_device(offset),
                device_id_type=pl.DeviceIdType.MESH,
            )
        )
        copies[-1].start()
    summed = terms_ref[...]
    for offset in range(1, pb_count):
        copies[offset - 1].wait()
        summed = summed + others_ref[offset - 1]
    out_ref[...] = summed[:fine] / (qpoints * pb_count * orbitals)


def axis_table(coords, places, cells):
    cell = jnp.arange(cells, dtype=jnp.int32) - cells // 2
    shift = coords[:, None] - places[None, :] * (FG // cells)
    index = (cell[:, None, None] * shift[None]) % FG
    angles = index.astype(jnp.float32) * (2.0 * math.pi / FG)
    return jnp.sum(jnp.cos(angles), 0) / cells, jnp.sum(jnp.sin(angles), 0) / cells


def times(first, second):
    return (
        first[0] * second[0] - first[1] * second[1],
        first[0] * second[1] + first[1] * second[0],
    )


def phase_table(fine_coords, points):
    first = axis_table(fine_coords[0], points // (GY * GZ), GX)
    second = axis_table(fine_coords[1], points // GZ % GY, GY)
    third = axis_table(fine_coords[2], points % GZ, GZ)
    return times(times(first, second), third)


def shards(
    coupling,
    gauge,
    kq_index,
    fine_coords,
    eig_right,
    eig_left,
    energy_k,
    energy_kq,
    occupied,
    frequency,
):
    points, qpoints, branches, orbitals, lanes = coupling.shape
    pb_count = lax.axis_size("pb")
    fine_total = fine_coords.shape[1]
    chunk = 16 if fine_total % 16 == 0 else fine_total
    chunks = fine_total // chunk
    padded = -(-points // 16) * 16
    params = pltpu.CompilerParams(vmem_limit_bytes=VMEM_LIMIT)

    all_gauge = lax.all_gather(gauge, "ka", axis=0, tiled=True)

    step = 4 if points % 4 == 0 else 1
    right = pl.pallas_call(
        right_kernel,
        grid=(points // step,),
        in_specs=[
            pl.BlockSpec((step, qpoints, branches, orbitals, lanes), lambda i: (i, 0, 0, 0, 0)),
            pl.BlockSpec((step, orbitals, lanes), lambda i: (i, 0, 0)),
        ],
        out_specs=pl.BlockSpec((step, qpoints, 2 * orbitals, 2 * lanes), lambda i: (i, 0, 0, 0)),
        out_shape=jax.ShapeDtypeStruct((points, qpoints, 2 * orbitals, 2 * lanes), jnp.bfloat16),
        compiler_params=params,
        cost_estimate=pl.CostEstimate(
            flops=8 * coupling.size * lanes, bytes_accessed=8 * coupling.size, transcendentals=0
        ),
        name="right_gauge",
    )(coupling, gauge)

    own_points = lax.axis_index("ka") * points + jnp.arange(points, dtype=jnp.int32)
    table_real, table_imag = phase_table(fine_coords, own_points)
    table = jnp.stack([table_real, table_imag]).reshape(2, chunks, chunk, points)
    table = table.transpose(1, 0, 2, 3).reshape(chunks, 2 * chunk, points)
    table = jnp.pad(table, ((0, 0), (0, 0), (0, padded - points)))
    own_rows = lax.dynamic_slice_in_dim(kq_index, lax.axis_index("pb") * qpoints, qpoints, 0)

    phonon = frequency.reshape(-1)
    scalars = jnp.stack([phonon, 1.0 / (jnp.exp(phonon / THERMAL) - 1.0), 1.0 / (2.0 * phonon)])
    shape = eig_left.shape
    energy_lanes = jnp.concatenate([energy_k, energy_k], 1)
    gap_lanes = jnp.broadcast_to(energy_kq[..., None], shape)
    filled_lanes = jnp.broadcast_to(occupied.astype(jnp.float32)[..., None], shape)

    ka_count = lax.axis_size("ka")
    fine_rows = eig_right.shape[0]
    fine_rows_padded = -(-fine_rows // 8) * 8
    partial_size = fine_total * branches * orbitals * lanes * 4 * qpoints
    power = ka_count & (ka_count - 1) == 0 and points % 2 == 0
    if chunks == 1 and power and ka_count > 2 and pb_count > 1 and partial_size <= 8 * 1024 * 1024:
        ka_others, pb_others = ka_count - 1, pb_count - 1
        vmem = pl.BlockSpec(memory_space=pltpu.VMEM)
        smem = pl.BlockSpec(memory_space=pltpu.SMEM)
        summed = pl.pallas_call(
            window_kernel,
            in_specs=[smem, smem, vmem, pl.BlockSpec(memory_space=pl.ANY)] + [vmem] * 6,
            out_specs=vmem,
            out_shape=jax.ShapeDtypeStruct((fine_rows, lanes), jnp.float32),
            scratch_shapes=[
                pltpu.VMEM((branches, orbitals, padded, lanes), jnp.float32),
                pltpu.VMEM((qpoints, fine_total, branches, orbitals, lanes), jnp.float32),
                pltpu.VMEM((qpoints, ka_others, fine_rows, branches, orbitals, lanes), jnp.float32),
                pltpu.VMEM((fine_rows, orbitals, lanes), jnp.float32),
                pltpu.VMEM((fine_rows_padded, lanes), jnp.float32),
                pltpu.VMEM((pb_others, fine_rows_padded, lanes), jnp.float32),
                pltpu.SemaphoreType.DMA((qpoints, ka_others)),
                pltpu.SemaphoreType.DMA((qpoints, ka_others)),
                pltpu.SemaphoreType.DMA((pb_others,)),
                pltpu.SemaphoreType.DMA((pb_others,)),
                pltpu.VMEM((ka_count * points, orbitals, lanes), jnp.float32),
                pltpu.VMEM(coupling.shape, jnp.float32),
                pltpu.VMEM((points, qpoints, 2 * orbitals, 2 * lanes), jnp.bfloat16),
                pltpu.SemaphoreType.DMA((2, ka_others)),
                pltpu.SemaphoreType.DMA((2, ka_others)),
                pltpu.SemaphoreType.DMA,
                pltpu.VMEM((qpoints, ka_count // 2, fine_rows, branches, orbitals, lanes), jnp.float32),
                pltpu.SemaphoreType.DMA((qpoints, ka_count // 2)),
                pltpu.SemaphoreType.DMA((qpoints, ka_count // 2)),
            ],
            compiler_params=pltpu.CompilerParams(
                vmem_limit_bytes=VMEM_LIMIT, collective_id=0, has_side_effects=True
            ),
            name="window",
        )(
            own_rows.reshape(-1), scalars, gauge, coupling, table[0], eig_right, eig_left,
            energy_lanes, gap_lanes, filled_lanes,
        )
        return summed[:, :orbitals]

    def one_qpoint(index, right_part, q):
        return pl.pallas_call(
            left_kernel,
            grid=(chunks,),
            in_specs=[
                pl.BlockSpec(memory_space=pltpu.SMEM),
                pl.BlockSpec(all_gauge.shape, lambda i: (0, 0, 0), pipeline_mode=pl.Buffered(1)),
                pl.BlockSpec((points, 1, 2 * orbitals, 2 * lanes), lambda i: (0, q, 0, 0)),
                pl.BlockSpec((1, 2 * chunk, padded), lambda i: (i, 0, 0)),
            ],
            out_specs=pl.BlockSpec((chunk, branches, orbitals, lanes), lambda i: (i, 0, 0, 0)),
            out_shape=jax.ShapeDtypeStruct((fine_total, branches, orbitals, lanes), jnp.float32),
            scratch_shapes=[pltpu.VMEM((branches, orbitals, padded, lanes), jnp.float32)],
            compiler_params=params,
            cost_estimate=pl.CostEstimate(
                flops=20_000_000_000, bytes_accessed=4 * all_gauge.size, transcendentals=0
            ),
            name="left_gauge",
        )(index, all_gauge, right_part, table)

    if chunks == 1:
        gathered = [
            lax.psum_scatter(one_qpoint(own_rows[q], right, q), "ka", scatter_dimension=0, tiled=True)
            for q in range(qpoints)
        ]
        coupled = jnp.stack(gathered, 1)
    else:

        def body(q, total):
            part = lax.dynamic_slice_in_dim(right, q, 1, 1)
            index = lax.dynamic_index_in_dim(own_rows, q, 0, keepdims=False)
            piece = lax.psum_scatter(
                one_qpoint(index, part, 0), "ka", scatter_dimension=0, tiled=True
            )
            return lax.dynamic_update_slice_in_dim(total, piece[:, None], q, 1)

        coupled = lax.fori_loop(
            0,
            qpoints,
            body,
            jnp.zeros((eig_right.shape[0], qpoints, branches, orbitals, lanes), jnp.float32),
        )

    contrib = pl.pallas_call(
        fine_kernel,
        in_specs=[pl.BlockSpec(memory_space=pltpu.SMEM)]
        + [pl.BlockSpec(memory_space=pltpu.VMEM)] * 6,
        out_specs=pl.BlockSpec(memory_space=pltpu.VMEM),
        out_shape=jax.ShapeDtypeStruct((eig_right.shape[0], lanes), jnp.float32),
        compiler_params=params,
        name="fine_terms",
    )(
        scalars,
        coupled,
        eig_right,
        eig_left,
        energy_lanes,
        gap_lanes,
        filled_lanes,
    )
    summed = lax.psum(contrib[:, :orbitals], "pb")
    return summed / (qpoints * pb_count * orbitals)


def solution(mesh):
    in_specs = (
        P("ka", "pb", None, None, None),
        P("ka", None, None),
        P(None, "ka"),
        P(),
        P("ka", None, None),
        P("ka", "pb", None, None),
        P("ka", None),
        P("ka", "pb", None),
        P("ka", "pb", None),
        P("pb", None),
    )
    out_specs = P("ka", None)
    return jax.shard_map(shards, mesh=mesh, in_specs=in_specs, out_specs=out_specs, check_vma=False)
```
